256 devices in a mesh: seq: 16 (over z, y_lo), mp: 16 (over x, y_hi, core).
Axes of the slice: x: 4, y: 4 (y_hi: 2, y_lo: 2; y = y_hi * 2 + y_lo), z: 8, core: 2. Of those that a mesh axis runs over, the one named last changes fastest.
Arguments:
- stream: bfloat16 [32768, 4096], P(('seq', 'mp')), may hold values from -6 to 6
- doc_start: int32 [32768], P(('seq', 'mp')), may hold values 0 or 1
- norm_gain: float32 [4096], replicated, may hold values from 0.1 to 1.9
- weight_in: bfloat16 [4096, 7168], P('seq', 'mp'), may hold values from -0.09375 to 0.09375
- weight_out: bfloat16 [7168, 4096], P('mp', 'seq'), may hold values from -0.0625 to 0.0625
- upstream: bfloat16 [32768, 4096], P(('seq', 'mp')), may hold values from -24 to 24
Outputs:
- mixed_stream: bfloat16 [32768, 4096], P(('seq', 'mp'))
- grad_stream: bfloat16 [32768, 4096], P(('seq', 'mp'))
- grad_gain: float32 [4096], replicated
- grad_weight_in: float32 [4096, 7168], P('seq', 'mp')
- grad_weight_out: float32 [7168, 4096], P('mp', 'seq')
The draws below stay inside these ranges and needn't reach their ends.
All inputs are finite; a program needn't handle non-finite values. No bound on the sum of `doc_start` on one device may be relied on, other than what follows from the above.
Results may differ from the reference program's by a relative error of at most 0.02.
Values may be sent and summed in bfloat16 or wider, within the bound.
No kernel may reach another device: no remote copies, remote signals or barrier semaphores. Data moves between devices by JAX's collectives and lax.ppermute only.
A program may use at most 128 MiB of HBM per device.

```python
import jax
import jax.numpy as jnp
from jax import lax

D = 4096
FF = 7168
TOKENS = 32768
GROUPS = 8192
N_SEQ = 16
N_MP = 16


def touch_ends(drawn, own_key, smallest, high):
    longest = drawn.shape.index(max(drawn.shape))
    spots = []
    for shift in (0, 1):
        where = [jax.random.randint(jax.random.fold_in(own_key, axis), (), 0, length) for axis, length in enumerate(drawn.shape)]
        where[longest] = (where[longest] + shift) % drawn.shape[longest]
        spots.append(tuple(where))
    return drawn.at[spots[0]].set(smallest).at[spots[1]].set(high)


def with_spikes(drawn, own_key, source, target, parts, factor):
    owner, partner = [(jnp.arange(drawn.shape[dim]) // (drawn.shape[dim] // parts)).reshape([-1 if axis == dim else 1 for axis in range(drawn.ndim)]) for dim in (source, target)]
    chosen = jax.random.permutation(own_key, parts)[partner]
    strong = (owner == chosen) | (owner == (partner + parts // 2) % parts)
    return jnp.where(strong, factor * drawn, drawn)


def shard_levels(own_key, shape, split, least, high):
    gain = 1.0
    for dim, parts in split:
        heights = jax.random.uniform(jax.random.fold_in(jax.random.fold_in(own_key, 6), dim), (parts,), jnp.float32, least / len(split), high / len(split))
        gain = gain * jnp.repeat(jnp.exp(heights), shape[dim] // parts).reshape((-1,) + (1,) * (len(shape) - 1 - dim))
    return gain


def normal_values(key, extent, deviation, reach, pieces=(), dtype=jnp.bfloat16):
    level = shard_levels(key, extent, pieces, -0.22, 0.18) if pieces else 1.0
    result = jax.random.normal(key, extent, jnp.float32) * deviation * level
    return jnp.minimum(jnp.maximum(result, -reach), reach).astype(dtype)


def noise_with(stream_key, extent, spread, reach, cuts, heavy, kind=jnp.bfloat16):
    entries = spread * jax.random.normal(stream_key, extent, jnp.float32)
    if cuts:
        entries = entries * shard_levels(stream_key, extent, cuts, -0.22, 0.18)
    return jnp.clip(with_spikes(entries, jax.random.fold_in(stream_key, 3), *heavy), -reach, reach).astype(kind)


def setup_inputs(seed: int = 0) -> dict:
    keys = jax.random.split(jax.random.key(seed), 7)
    stream = normal_values(keys[0], (TOKENS, D), 1.0, 6.0, ((0, 256),))
    doc_start = touch_ends((jax.random.randint(keys[1], (TOKENS,), 0, 32) < 1).astype(jnp.int32), jax.random.fold_in(keys[1], 1), 0, 1)
    norm_gain = jnp.clip(1.0 + 0.18 * jax.random.normal(keys[2], (D,), jnp.float32), 0.1, 1.9)
    weight_in = normal_values(keys[3], (D, FF), D ** -0.5, 0.09375, ((0, 16), (1, 16)))
    weight_out = normal_values(keys[4], (FF, D), FF ** -0.5, 0.0625, ((0, 16), (1, 16)))
    upstream = noise_with(keys[5], (TOKENS, D), 1.0, 24.0, ((0, 256),), (0, 1, 256, 6.0))
    return dict(stream=stream, doc_start=doc_start, norm_gain=norm_gain, weight_in=weight_in, weight_out=weight_out, upstream=upstream)


def rounded(tensor):
    return lax.optimization_barrier(tensor.astype(jnp.bfloat16)).astype(jnp.float32)

def gelu_tanh(tensor):
    return jax.nn.gelu(tensor, approximate=True)

def contract(left, right, left_dim, right_dim):
    return lax.dot_general(left, right, (((left_dim,), (right_dim,)), ((), ())), preferred_element_type=jnp.float32)

def reference(stream, doc_start, norm_gain, weight_in, weight_out, upstream):
    feat_width = stream.shape[1]
    grouped = stream.reshape(GROUPS, 4, feat_width).astype(jnp.float32)
    pooled = (lax.optimization_barrier(jnp.sum(grouped, axis=1)) * 0.25).astype(jnp.bfloat16)
    pooled_f = pooled.astype(jnp.float32)
    inv_rms = lax.rsqrt(lax.optimization_barrier(jnp.mean(pooled_f * pooled_f, axis=1, keepdims=True)) + 1e-05)
    normed = (pooled_f * inv_rms * norm_gain).astype(jnp.bfloat16)
    hidden_pre = jnp.dot(normed, weight_in, preferred_element_type=jnp.float32)
    activated = gelu_tanh(hidden_pre).astype(jnp.bfloat16)
    ff_block = FF // N_MP
    down_sum = jnp.zeros((GROUPS, feat_width), jnp.float32)
    for position in range(N_MP):
        lower = position * ff_block
        down_sum = down_sum + rounded(jnp.dot(activated[:, lower:lower + ff_block], weight_out[lower:lower + ff_block], preferred_element_type=jnp.float32))
    coarse = (pooled_f + down_sum).astype(jnp.bfloat16)
    starts = doc_start.reshape(GROUPS, 4).astype(jnp.float32)
    keep_mask = jnp.cumprod(1.0 - starts, axis=1)
    keep_mask = keep_mask * (jnp.arange(GROUPS) > 0).astype(jnp.float32)[:, None]
    earlier = jnp.concatenate([jnp.zeros((1, feat_width), jnp.bfloat16), coarse[:-1]], axis=0)
    mixed_stream = (grouped + keep_mask[:, :, None] * earlier.astype(jnp.float32)[:, None, :]).reshape(TOKENS, feat_width).astype(jnp.bfloat16)
    up_grouped = upstream.reshape(GROUPS, 4, feat_width).astype(jnp.float32)
    group_sums = lax.optimization_barrier(jnp.sum(up_grouped * keep_mask[:, :, None], axis=1))
    grad_coarse = jnp.concatenate([group_sums[1:], jnp.zeros((1, feat_width), jnp.float32)], axis=0).astype(jnp.bfloat16)
    grad_act = contract(grad_coarse, weight_out, 1, 1)
    pullback = jax.vjp(gelu_tanh, hidden_pre)[1]
    grad_pre = pullback(grad_act)[0].astype(jnp.bfloat16)
    row_block = GROUPS // N_SEQ
    grad_weight_out = jnp.zeros((FF, feat_width), jnp.float32)
    grad_weight_in = jnp.zeros((feat_width, FF), jnp.float32)
    for position in range(N_SEQ):
        lower = position * row_block
        grad_weight_out = grad_weight_out + rounded(contract(activated[lower:lower + row_block], grad_coarse[lower:lower + row_block], 0, 0))
        grad_weight_in = grad_weight_in + rounded(contract(normed[lower:lower + row_block], grad_pre[lower:lower + row_block], 0, 0))
    grad_normed = jnp.zeros((GROUPS, feat_width), jnp.float32)
    for position in range(N_MP):
        lower = position * ff_block
        grad_normed = grad_normed + rounded(contract(grad_pre[:, lower:lower + ff_block], weight_in[:, lower:lower + ff_block], 1, 1))
    grad_gain = lax.optimization_barrier(jnp.sum(grad_normed * pooled_f * inv_rms, axis=0))
    scaled = norm_gain * grad_normed
    grad_pooled = grad_coarse.astype(jnp.float32) + inv_rms * (scaled - pooled_f * inv_rms * inv_rms * lax.optimization_barrier(jnp.mean(scaled * pooled_f, axis=1, keepdims=True)))
    grad_stream = (up_grouped + 0.25 * grad_pooled[:, None, :]).reshape(TOKENS, feat_width).astype(jnp.bfloat16)
    return (mixed_stream, grad_stream, grad_gain, grad_weight_in, grad_weight_out)
```

```python
import functools

import jax
import jax.numpy as jnp
from jax import lax
from jax.experimental import pallas as pl
from jax.experimental.pallas import tpu as pltpu
from jax.sharding import Mesh, PartitionSpec as P

AXES = ("z", "yl", "x", "yh", "c")
NZ, NY, NX = 8, 4, 4


def linear(z, y, x, c):
    return (((z * 2 + y % 2) * NX + x) * 2 + y // 2) * 2 + c


def places():
    return [
        (z, y, x, c) for z in range(NZ) for y in range(NY) for x in range(NX) for c in range(2)
    ]


def shift(value, dx=0, dy=0):
    pairs = [
        (linear(z, y, x, c), linear(z, (y + dy) % NY, (x + dx) % NX, c)) for z, y, x, c in places()
    ]
    return lax.ppermute(value, AXES, pairs)


def other_core(value):
    pairs = [(linear(z, y, x, c), linear(z, y, x, 1 - c)) for z, y, x, c in places()]
    return lax.ppermute(value, AXES, pairs)


def swap_low(value):
    pairs = [
        (linear(z, y, x, c), linear(z, (y // 2) * 2 + c, x, y % 2)) for z, y, x, c in places()
    ]
    return lax.ppermute(value, AXES, pairs)


def from_behind(value, by):
    count = NZ * NY * NX * 2
    pairs = [(i, i + by) for i in range(count) if 0 <= i + by < count]
    return lax.ppermute(value, AXES, pairs)


def nt(a, b):
    return lax.dot_general(a, b, (((1,), (1,)), ((), ())), preferred_element_type=jnp.float32)


def nn(a, b):
    return jnp.dot(a, b, preferred_element_type=jnp.float32)


def block_kernel(n_blocks, chunks, *refs):
    acts = refs[:n_blocks]
    w_own, w_oth = refs[n_blocks : n_blocks + 2]
    outs = refs[n_blocks + 2 : 2 * n_blocks + 2]
    g_own, g_oth, gain = refs[2 * n_blocks + 2 : 2 * n_blocks + 5]
    (p_s, g_s, wi_s, wo_s, d_s, n_s, gi_s, go_s, h_s, ga_s, sq_s, act, gp, act_t, gp_t, in_sem,
     out_sem) = refs[2 * n_blocks + 5 :]
    core = lax.axis_index("c")
    rows = acts[0].shape[1]
    hidden = wi_s.shape[0]
    half = w_own.shape[2]
    width = 2 * half
    feats = chunks * width

    def cols(z):
        return pl.ds(pl.multiple_of(z * width, width), width)

    def w_cols(z, which):
        return pl.ds(pl.multiple_of(z * width + which * half, half), half)

    def fetch(z, carry):
        for i in range(n_blocks):
            at = pl.ds(i * rows, rows)
            pltpu.make_async_copy(
                acts[i].at[0, :, cols(z)], p_s.at[at, cols(z)], in_sem.at[0, z]
            ).start()
            pltpu.make_async_copy(
                acts[i].at[1, :, cols(z)], g_s.at[at, cols(z)], in_sem.at[1, z]
            ).start()
        for source, which in ((w_own, core), (w_oth, 1 - core)):
            pltpu.make_async_copy(
                source.at[z, pl.ds(0, hidden), :], wi_s.at[:, w_cols(z, which)], in_sem.at[2, z]
            ).start()
            pltpu.make_async_copy(
                source.at[z, pl.ds(hidden, hidden), :],
                wo_s.at[:, w_cols(z, which)],
                in_sem.at[3, z],
            ).start()
        return carry

    lax.fori_loop(0, chunks, fetch, 0)
    h_s[...] = jnp.zeros_like(h_s)
    ga_s[...] = jnp.zeros_like(ga_s)
    sq_s[...] = jnp.zeros_like(sq_s)

    def first(z, carry):
        for k, buf in enumerate((p_s, g_s, wi_s, wo_s)):
            view = buf.at[:, cols(z)]
            pltpu.make_async_copy(view, view, in_sem.at[k, z]).wait()
        p = p_s[:, cols(z)]
        h_s[...] += nt(p, wi_s[:, cols(z)])
        ga_s[...] += nt(g_s[:, cols(z)], wo_s[:, cols(z)])
        pf = p.astype(jnp.float32)
        sq_s[...] += jnp.sum(pf * pf, axis=1, keepdims=True)
        return carry

    lax.fori_loop(0, chunks, first, 0)
    inv = lax.rsqrt(sq_s[...] * (1.0 / feats) + 1e-05)
    v = h_s[...] * inv
    v2 = v * v
    t = jnp.tanh(0.7978845608 * v * (1.0 + 0.044715 * v2))
    up = 0.5 * (1.0 + t)
    a = (v * up).astype(jnp.bfloat16)
    slope = up + 0.5 * v * (1.0 - t * t) * (0.7978845608 * (1.0 + 0.134145 * v2))
    b = (ga_s[...] * slope * inv).astype(jnp.bfloat16)
    act[...] = a
    gp[...] = b
    act_t[...] = a.T
    gp_t[...] = b.T

    def second(z, carry):
        wi = wi_s[:, cols(z)]
        d_s[:, cols(z)] = nn(act[...], wo_s[:, cols(z)]).astype(jnp.bfloat16)
        n_s[:, cols(z)] = nn(gp[...], wi).astype(jnp.bfloat16)
        go_s[:, cols(z)] = nn(act_t[...], g_s[:, cols(z)]).astype(jnp.bfloat16)
        gi = nn(gp_t[...], p_s[:, cols(z)])
        gi_s[:, cols(z)] = gi.astype(jnp.bfloat16)
        gain[:, cols(z)] = jnp.sum(gi * wi.astype(jnp.float32), axis=0, keepdims=True)
        for i in range(n_blocks):
            at = pl.ds(i * rows, rows)
            pltpu.make_async_copy(
                d_s.at[at, cols(z)], outs[i].at[0, :, cols(z)], out_sem.at[0, z]
            ).start()
            pltpu.make_async_copy(
                n_s.at[at, cols(z)], outs[i].at[1, :, cols(z)], out_sem.at[1, z]
            ).start()
        for dest, which in ((g_own, core), (g_oth, 1 - core)):
            pltpu.make_async_copy(
                gi_s.at[:, w_cols(z, which)], dest.at[z, pl.ds(0, hidden), :], out_sem.at[2, z]
            ).start()
            pltpu.make_async_copy(
                go_s.at[:, w_cols(z, which)], dest.at[z, pl.ds(hidden, hidden), :], out_sem.at[3, z]
            ).start()
        return carry

    lax.fori_loop(0, chunks, second, 0)

    def drain(z, carry):
        for k, buf in enumerate((d_s, n_s, gi_s, go_s)):
            view = buf.at[:, cols(z)]
            pltpu.make_async_copy(view, view, out_sem.at[k, z]).wait()
        return carry

    lax.fori_loop(0, chunks, drain, 0)


def block(acts, w_own, w_oth):
    n = len(acts)
    _, rows, feats = acts[0].shape
    chunks, hidden2, half = w_own.shape
    hidden = hidden2 // 2
    total = n * rows
    bf = jnp.bfloat16
    anywhere = pl.BlockSpec(memory_space=pl.ANY)
    flops = 12 * total * feats * hidden
    return pl.pallas_call(
        functools.partial(block_kernel, n, chunks),
        out_shape=[jax.ShapeDtypeStruct(acts[0].shape, bf)] * n
        + [jax.ShapeDtypeStruct(w_own.shape, bf)] * 2
        + [jax.ShapeDtypeStruct((1, feats), jnp.float32)],
        in_specs=[anywhere] * (n + 2),
        out_specs=[anywhere] * (n + 2) + [pl.BlockSpec(memory_space=pltpu.VMEM)],
        scratch_shapes=[pltpu.VMEM((total, feats), bf)] * 2
        + [pltpu.VMEM((hidden, feats), bf)] * 2
        + [pltpu.VMEM((total, feats), bf)] * 2
        + [pltpu.VMEM((hidden, feats), bf)] * 2
        + [pltpu.VMEM((total, hidden), jnp.float32)] * 2
        + [pltpu.VMEM((total, 1), jnp.float32)]
        + [pltpu.VMEM((total, hidden), bf)] * 2
        + [pltpu.VMEM((hidden, total), bf)] * 2
        + [pltpu.SemaphoreType.DMA((4, chunks)), pltpu.SemaphoreType.DMA((4, chunks))],
        compiler_params=pltpu.CompilerParams(vmem_limit_bytes=48 * 1024 * 1024),
        cost_estimate=pl.CostEstimate(
            flops=flops, bytes_accessed=8 * (total + hidden) * feats * 2, transcendentals=0
        ),
    )(*acts, w_own, w_oth)


def gather_plane(first, second):
    a = jnp.concatenate([first] + [shift(first, dy=d) for d in (1, 2, 3)], axis=1)
    b = jnp.concatenate([second] + [shift(second, dx=d) for d in (1, 2, 3)], axis=1)
    return [a] + [shift(a, dx=d) for d in (1, 2, 3)] + [b] + [shift(b, dy=d) for d in (1, 2, 3)]


def add_all(parts):
    total = parts[0].astype(jnp.float32)
    for part in parts[1:]:
        total = total + part.astype(jnp.float32)
    return total


def scatter_plane(blocks, rows):
    a = add_all([blocks[0]] + [shift(blocks[d], dx=-d) for d in (1, 2, 3)]).astype(jnp.bfloat16)
    b = add_all([blocks[4]] + [shift(blocks[4 + d], dy=-d) for d in (1, 2, 3)]).astype(jnp.bfloat16)
    a = [a[:, d * rows : (d + 1) * rows] for d in range(4)]
    b = [b[:, d * rows : (d + 1) * rows] for d in range(4)]
    a = add_all([a[0]] + [shift(a[d], dy=-d) for d in (1, 2, 3)])
    b = add_all([b[0]] + [shift(b[d], dx=-d) for d in (1, 2, 3)])
    return jnp.concatenate([a, b], axis=1)


def shards(stream, doc_start, norm_gain, weight_in, weight_out, upstream):
    tok_rows, feats = stream.shape
    groups = tok_rows // 4
    hidden = weight_out.shape[0]
    k_rows = weight_in.shape[0]
    bf = jnp.bfloat16
    seq = lax.axis_index("z") * 2 + lax.axis_index("yl")
    gain = lax.dynamic_slice(norm_gain, (seq * k_rows,), (k_rows,))

    scaled_in = (weight_in.T.astype(jnp.float32) * gain[None, :]).astype(bf)
    both = swap_low(jnp.concatenate([scaled_in, weight_out], axis=0))
    w_own = lax.all_gather(both, "z", axis=0, tiled=False)

    starts = doc_start.reshape(groups, 4).astype(jnp.float32)
    keep = jnp.cumprod(1.0 - starts, axis=1).reshape(tok_rows)
    group_of = lax.broadcasted_iota(jnp.int32, (groups, tok_rows), 1) // 4
    here = lax.broadcasted_iota(jnp.int32, (groups, tok_rows), 0)
    pool = jnp.where(group_of == here, 0.25, 0.0).astype(bf)
    pooled = nn(pool, stream).astype(bf)
    pick = jnp.where(group_of == here, keep[None, :], 0.0).astype(bf)
    group_sums = nn(pick, upstream).astype(bf)
    following = from_behind(group_sums[:1], -1)
    grad_coarse = jnp.concatenate([group_sums[1:], following], axis=0)

    acts = jnp.stack([pooled, grad_coarse], axis=0)
    rows = groups // 2
    blocks = gather_plane(acts[:, :rows], acts[:, rows:])
    w_oth = other_core(w_own)
    results = block(blocks, w_own, w_oth)
    outs, (g_own, g_oth, gain_part) = results[:8], results[8:]

    mine = (g_own.astype(jnp.float32) + other_core(g_oth).astype(jnp.float32)).astype(bf)
    grads = swap_low(lax.psum_scatter(mine, "z", scatter_dimension=0, tiled=False))
    grad_weight_in = (grads[:hidden].astype(jnp.float32) * gain[None, :]).T
    grad_weight_out = grads[hidden:].astype(jnp.float32)
    grad_gain = lax.psum(gain_part[0] / norm_gain, AXES)

    down_sum, scaled = scatter_plane(outs, rows)
    pooled_f = pooled.astype(jnp.float32)
    inv_sq = 1.0 / (jnp.mean(pooled_f * pooled_f, axis=1, keepdims=True) + 1e-05)
    coarse = (pooled_f + down_sum).astype(bf)
    carried = from_behind(coarse[groups - 1 :], 1)
    earlier = jnp.concatenate([carried, coarse[:-1]], axis=0)
    mixed_stream = (stream.astype(jnp.float32) + nn(pick.T, earlier)).astype(bf)
    grad_pooled = grad_coarse.astype(jnp.float32) + (
        scaled - pooled_f * inv_sq * jnp.mean(scaled * pooled_f, axis=1, keepdims=True)
    )
    grad_stream = (upstream.astype(jnp.float32) + nn(pool.T, grad_pooled.astype(bf))).astype(bf)
    return (mixed_stream, grad_stream, grad_gain, grad_weight_in, grad_weight_out)


def solution(mesh):
    fine = Mesh(mesh.devices.reshape(NZ, 2, NX, 2, 2), AXES)
    rows = P(AXES, None)
    seq, mp = ("z", "yl"), ("x", "yh", "c")
    in_specs = (rows, P(AXES), P(), P(seq, mp), P(mp, seq), rows)
    out_specs = (rows, rows, P(), P(seq, mp), P(mp, seq))
    return jax.shard_map(shards, mesh=fine, in_specs=in_specs, out_specs=out_specs, check_vma=False)
```

```python
import functools

import jax
import jax.numpy as jnp
from jax import lax
from jax.experimental import pallas as pl
from jax.experimental.pallas import tpu as pltpu
from jax.sharding import Mesh, PartitionSpec as P

AXES = ("z", "yl", "x", "yh", "c")
NZ, NY, NX = 8, 4, 4


def linear(z, y, x, c):
    return (((z * 2 + y % 2) * NX + x) * 2 + y // 2) * 2 + c


def places():
    return [
        (z, y, x, c) for z in range(NZ) for y in range(NY) for x in range(NX) for c in range(2)
    ]


def shift(value, dx=0, dy=0):
    pairs = [
        (linear(z, y, x, c), linear(z, (y + dy) % NY, (x + dx) % NX, c)) for z, y, x, c in places()
    ]
    return lax.ppermute(value, AXES, pairs)


def other_core(value):
    pairs = [(linear(z, y, x, c), linear(z, y, x, 1 - c)) for z, y, x, c in places()]
    return lax.ppermute(value, AXES, pairs)


def swap_low(value):
    pairs = [
        (linear(z, y, x, c), linear(z, (y // 2) * 2 + c, x, y % 2)) for z, y, x, c in places()
    ]
    return lax.ppermute(value, AXES, pairs)


def from_behind(value, by):
    count = NZ * NY * NX * 2
    pairs = [(i, i + by) for i in range(count) if 0 <= i + by < count]
    return lax.ppermute(value, AXES, pairs)


def nt(a, b):
    return lax.dot_general(a, b, (((1,), (1,)), ((), ())), preferred_element_type=jnp.float32)


def nn(a, b):
    return jnp.dot(a, b, preferred_element_type=jnp.float32)


def slots(refs):
    s0, s1, p2, g2, s3 = refs
    return [(s0.at[0], s0.at[1]), (s1.at[0], s1.at[1]), (p2, g2), (s3.at[0], s3.at[1])]


def block_kernel(chunks, *refs):
    acts = slots(refs[:5]) + slots(refs[5:10])
    w_own, w_oth = refs[10:12]
    outs = slots(refs[12:17]) + slots(refs[17:22])
    g_own, g_oth, gain = refs[22:25]
    (p_s, g_s, wi_s, wo_s, d_s, n_s, gi_s, go_s, h_s, ga_s, sq_s, act, gp, act_t, gp_t, in_sem,
     out_sem) = refs[25:]
    core = lax.axis_index("c")
    rows = refs[0].shape[1]
    hidden = wi_s.shape[0]
    half = w_own.shape[2]
    width = 2 * half
    feats = chunks * width

    def cols(z):
        return pl.ds(pl.multiple_of(z * width, width), width)

    def w_cols(z, which):
        return pl.ds(pl.multiple_of(z * width + which * half, half), half)

    def fetch(z, carry):
        for i, pair in enumerate(acts):
            at = pl.ds(i * rows, rows)
            for k, (source, buf) in enumerate(zip(pair, (p_s, g_s))):
                pltpu.make_async_copy(
                    source.at[:, cols(z)], buf.at[at, cols(z)], in_sem.at[k, z]
                ).start()
        for source, which in ((w_own, core), (w_oth, 1 - core)):
            pltpu.make_async_copy(
                source.at[z, pl.ds(0, hidden), :], wi_s.at[:, w_cols(z, which)], in_sem.at[2, z]
            ).start()
            pltpu.make_async_copy(
                source.at[z, pl.ds(hidden, hidden), :],
                wo_s.at[:, w_cols(z, which)],
                in_sem.at[3, z],
            ).start()
        return carry

    lax.fori_loop(0, chunks, fetch, 0)
    h_s[...] = jnp.zeros_like(h_s)
    ga_s[...] = jnp.zeros_like(ga_s)
    sq_s[...] = jnp.zeros_like(sq_s)

    def first(z, carry):
        for k, buf in enumerate((p_s, g_s, wi_s, wo_s)):
            view = buf.at[:, cols(z)]
            pltpu.make_async_copy(view, view, in_sem.at[k, z]).wait()
        p = p_s[:, cols(z)]
        h_s[...] += nt(p, wi_s[:, cols(z)])
        ga_s[...] += nt(g_s[:, cols(z)], wo_s[:, cols(z)])
        pf = p.astype(jnp.float32)
        sq_s[...] += jnp.sum(pf * pf, axis=1, keepdims=True)
        return carry

    lax.fori_loop(0, chunks, first, 0)
    inv = lax.rsqrt(sq_s[...] * (1.0 / feats) + 1e-05)
    v = h_s[...] * inv
    v2 = v * v
    t = jnp.tanh(0.7978845608 * v * (1.0 + 0.044715 * v2))
    up = 0.5 * (1.0 + t)
    a = (v * up).astype(jnp.bfloat16)
    slope = up + 0.5 * v * (1.0 - t * t) * (0.7978845608 * (1.0 + 0.134145 * v2))
    b = (ga_s[...] * slope * inv).astype(jnp.bfloat16)
    act[...] = a
    gp[...] = b
    act_t[...] = a.T
    gp_t[...] = b.T

    def second(z, carry):
        wi = wi_s[:, cols(z)]
        d_s[:, cols(z)] = nn(act[...], wo_s[:, cols(z)]).astype(jnp.bfloat16)
        n_s[:, cols(z)] = nn(gp[...], wi).astype(jnp.bfloat16)
        go_s[:, cols(z)] = nn(act_t[...], g_s[:, cols(z)]).astype(jnp.bfloat16)
        gi = nn(gp_t[...], p_s[:, cols(z)])
        gi_s[:, cols(z)] = gi.astype(jnp.bfloat16)
        gain[:, cols(z)] = jnp.sum(gi * wi.astype(jnp.float32), axis=0, keepdims=True)
        for i, pair in enumerate(outs):
            at = pl.ds(i * rows, rows)
            for k, (dest, buf) in enumerate(zip(pair, (d_s, n_s))):
                pltpu.make_async_copy(
                    buf.at[at, cols(z)], dest.at[:, cols(z)], out_sem.at[k, z]
                ).start()
        for dest, which in ((g_own, core), (g_oth, 1 - core)):
            pltpu.make_async_copy(
                gi_s.at[:, w_cols(z, which)], dest.at[z, pl.ds(0, hidden), :], out_sem.at[2, z]
            ).start()
            pltpu.make_async_copy(
                go_s.at[:, w_cols(z, which)], dest.at[z, pl.ds(hidden, hidden), :], out_sem.at[3, z]
            ).start()
        return carry

    lax.fori_loop(0, chunks, second, 0)

    def drain(z, carry):
        for k, buf in enumerate((d_s, n_s, gi_s, go_s)):
            view = buf.at[:, cols(z)]
            pltpu.make_async_copy(view, view, out_sem.at[k, z]).wait()
        return carry

    lax.fori_loop(0, chunks, drain, 0)


def block(acts, w_own, w_oth):
    _, rows, feats = acts[0].shape
    chunks, hidden2, half = w_own.shape
    hidden = hidden2 // 2
    total = 8 * rows
    bf = jnp.bfloat16
    anywhere = pl.BlockSpec(memory_space=pl.ANY)
    flops = 12 * total * feats * hidden
    return pl.pallas_call(
        functools.partial(block_kernel, chunks),
        out_shape=[jax.ShapeDtypeStruct(act.shape, bf) for act in acts]
        + [jax.ShapeDtypeStruct(w_own.shape, bf)] * 2
        + [jax.ShapeDtypeStruct((1, feats), jnp.float32)],
        in_specs=[anywhere] * 12,
        out_specs=[anywhere] * 12 + [pl.BlockSpec(memory_space=pltpu.VMEM)],
        scratch_shapes=[pltpu.VMEM((total, feats), bf)] * 2
        + [pltpu.VMEM((hidden, feats), bf)] * 2
        + [pltpu.VMEM((total, feats), bf)] * 2
        + [pltpu.VMEM((hidden, feats), bf)] * 2
        + [pltpu.VMEM((total, hidden), jnp.float32)] * 2
        + [pltpu.VMEM((total, 1), jnp.float32)]
        + [pltpu.VMEM((total, hidden), bf)] * 2
        + [pltpu.VMEM((hidden, total), bf)] * 2
        + [pltpu.SemaphoreType.DMA((4, chunks)), pltpu.SemaphoreType.DMA((4, chunks))],
        compiler_params=pltpu.CompilerParams(vmem_limit_bytes=48 * 1024 * 1024),
        cost_estimate=pl.CostEstimate(
            flops=flops, bytes_accessed=8 * (total + hidden) * feats * 2, transcendentals=0
        ),
    )(*acts, w_own, w_oth)


def add_all(parts):
    total = parts[0].astype(jnp.float32)
    for part in parts[1:]:
        total = total + part.astype(jnp.float32)
    return total


def by_x(value, d):
    return shift(value, dx=d)


def by_y(value, d):
    return shift(value, dy=d)


def gather_plane(first, second):
    a = jnp.concatenate([first] + [by_y(first, d) for d in (1, 2, 3)], axis=1)
    b = jnp.concatenate([second] + [by_x(second, d) for d in (1, 2, 3)], axis=1)
    a, b = lax.optimization_barrier((a, b))
    a1, a3, b1, b3 = by_x(a, 1), by_x(a, -1), by_y(b, 1), by_y(b, -1)
    a2, b2 = (by_x(a1[0], 1), by_x(a3[1], -1)), (by_y(b1[0], 1), by_y(b3[1], -1))
    return [a, a1, *a2, a3, b, b1, *b2, b3], (a, b)


def fold(half, move):
    s0, s1, d2, n2, s3 = half
    bf = jnp.bfloat16
    d2, n2 = move(d2, -1), move(n2, 1)
    s1 = jnp.stack([add_all([s1[0], d2]).astype(bf), s1[1]])
    s3 = jnp.stack([s3[0], add_all([s3[1], n2]).astype(bf)])
    return s1, s3


def scatter_plane(outs, rows, gain_part, weight_part):
    sends = (*fold(outs[:5], by_x), *fold(outs[5:], by_y), gain_part, weight_part)
    a1, a3, b1, b3, gain_part, weight_part = lax.optimization_barrier(sends)
    weight_sum = lax.psum_scatter(weight_part, "z", scatter_dimension=0, tiled=False)
    a1, a3, b1, b3 = by_x(a1, -1), by_x(a3, 1), by_y(b1, -1), by_y(b3, 1)
    arrived = (a1, a3, b1, b3, total_over_all(gain_part), weight_sum)
    a1, a3, b1, b3, grad_gain, weight_sum = lax.optimization_barrier(arrived)
    a = add_all([outs[0], a1, a3]).astype(jnp.bfloat16)
    b = add_all([outs[5], b1, b3]).astype(jnp.bfloat16)
    a = [a[:, d * rows : (d + 1) * rows] for d in range(4)]
    b = [b[:, d * rows : (d + 1) * rows] for d in range(4)]
    a = add_all([a[0]] + [by_y(a[d], -d) for d in (1, 2, 3)])
    b = add_all([b[0]] + [by_x(b[d], -d) for d in (1, 2, 3)])
    return jnp.concatenate([a, b], axis=1), grad_gain, weight_sum


def total_over_all(value):
    moves = [lambda p, k=k: (p[0] ^ k, p[1], p[2], p[3]) for k in (1, 2, 4)]
    moves += [lambda p: (p[0], p[1], p[2], 1 - p[3])]
    moves += [lambda p, k=k: (p[0], p[1] ^ k, p[2], p[3]) for k in (1, 2)]
    moves += [lambda p, k=k: (p[0], p[1], p[2] ^ k, p[3]) for k in (1, 2)]
    for move in moves:
        value = value + lax.ppermute(
            value, AXES, [(linear(*p), linear(*move(p))) for p in places()]
        )
    return value


def shards(stream, doc_start, norm_gain, weight_in, weight_out, upstream):
    tok_rows, feats = stream.shape
    groups = tok_rows // 4
    hidden = weight_out.shape[0]
    k_rows = weight_in.shape[0]
    bf = jnp.bfloat16
    seq = lax.axis_index("z") * 2 + lax.axis_index("yl")
    gain = lax.dynamic_slice(norm_gain, (seq * k_rows,), (k_rows,))

    scaled_in = (weight_in.T.astype(jnp.float32) * gain[None, :]).astype(bf)
    both = swap_low(jnp.concatenate([scaled_in, weight_out], axis=0))
    w_own = lax.all_gather(both, "z", axis=0, tiled=False)

    starts = doc_start.reshape(groups, 4).astype(jnp.float32)
    keep = jnp.cumprod(1.0 - starts, axis=1).reshape(tok_rows)
    group_of = lax.broadcasted_iota(jnp.int32, (groups, tok_rows), 1) // 4
    here = lax.broadcasted_iota(jnp.int32, (groups, tok_rows), 0)
    pool = jnp.where(group_of == here, 0.25, 0.0).astype(bf)
    pooled = nn(pool, stream).astype(bf)
    pick = jnp.where(group_of == here, keep[None, :], 0.0).astype(bf)
    group_sums = nn(pick, upstream).astype(bf)
    following = from_behind(group_sums[:1], -1)
    grad_coarse = jnp.concatenate([group_sums[1:], following], axis=0)

    acts = jnp.stack([pooled, grad_coarse], axis=0)
    rows = groups // 2
    blocks, begun = gather_plane(acts[:, :rows], acts[:, rows:])
    w_own = lax.optimization_barrier((w_own, *begun))[0]
    w_oth = other_core(w_own)
    results = block(blocks, w_own, w_oth)
    outs, (g_own, g_oth, gain_part) = results[:10], results[10:]

    mine = (g_own.astype(jnp.float32) + other_core(g_oth).astype(jnp.float32)).astype(bf)
    (down_sum, scaled), grad_gain, grads = scatter_plane(outs, rows, gain_part[0] / norm_gain, mine)
    grads = swap_low(grads)
    grad_weight_in = (grads[:hidden].astype(jnp.float32) * gain[None, :]).T
    grad_weight_out = grads[hidden:].astype(jnp.float32)
    pooled_f = pooled.astype(jnp.float32)
    inv_sq = 1.0 / (jnp.mean(pooled_f * pooled_f, axis=1, keepdims=True) + 1e-05)
    coarse = (pooled_f + down_sum).astype(bf)
    carried = from_behind(coarse[groups - 1 :], 1)
    earlier = jnp.concatenate([carried, coarse[:-1]], axis=0)
    mixed_stream = (stream.astype(jnp.float32) + nn(pick.T, earlier)).astype(bf)
    grad_pooled = grad_coarse.astype(jnp.float32) + (
        scaled - pooled_f * inv_sq * jnp.mean(scaled * pooled_f, axis=1, keepdims=True)
    )
    grad_stream = (upstream.astype(jnp.float32) + nn(pool.T, grad_pooled.astype(bf))).astype(bf)
    return (mixed_stream, grad_stream, grad_gain, grad_weight_in, grad_weight_out)


def solution(mesh):
    fine = Mesh(mesh.devices.reshape(NZ, 2, NX, 2, 2), AXES)
    rows = P(AXES, None)
    seq, mp = ("z", "yl"), ("x", "yh", "c")
    in_specs = (rows, P(AXES), P(), P(seq, mp), P(mp, seq), rows)
    out_specs = (rows, rows, P(), P(seq, mp), P(mp, seq))
    return jax.shard_map(shards, mesh=fine, in_specs=in_specs, out_specs=out_specs, check_vma=False)
```

```python
import functools

import jax
import jax.numpy as jnp
from jax import lax
from jax.experimental import pallas as pl
from jax.experimental.pallas import tpu as pltpu
from jax.sharding import Mesh, PartitionSpec as P

AXES = ("z", "yl", "x", "yh", "c")
NZ, NY, NX = 8, 4, 4


def linear(z, y, x, c):
    return (((z * 2 + y % 2) * NX + x) * 2 + y // 2) * 2 + c


def places():
    return [
        (z, y, x, c) for z in range(NZ) for y in range(NY) for x in range(NX) for c in range(2)
    ]


def shift(value, first=0, second=0):
    pairs = []
    for z, y, x, c in places():
        dy, dx = (second, first) if c else (first, second)
        pairs.append((linear(z, y, x, c), linear(z, (y + dy) % NY, (x + dx) % NX, c)))
    return lax.ppermute(value, AXES, pairs)


def other_core(value):
    pairs = [(linear(z, y, x, c), linear(z, y, x, 1 - c)) for z, y, x, c in places()]
    return lax.ppermute(value, AXES, pairs)


def swap_low(value):
    pairs = [
        (linear(z, y, x, c), linear(z, (y // 2) * 2 + c, x, y % 2)) for z, y, x, c in places()
    ]
    return lax.ppermute(value, AXES, pairs)


def from_behind(value, by):
    count = NZ * NY * NX * 2
    pairs = [(i, i + by) for i in range(count) if 0 <= i + by < count]
    return lax.ppermute(value, AXES, pairs)


def nt(a, b):
    return lax.dot_general(a, b, (((1,), (1,)), ((), ())), preferred_element_type=jnp.float32)


def nn(a, b):
    return jnp.dot(a, b, preferred_element_type=jnp.float32)


def block_kernel(chunks, *refs):
    acts = list(zip(refs[:4], refs[4:8]))
    w_own, w_oth = refs[8:10]
    outs = list(zip(refs[10:14], refs[14:18]))
    g_own, g_oth, gain = refs[18:21]
    (p_s, g_s, wi_s, wo_s, d_s, n_s, gi_s, go_s, h_s, ga_s, sq_s, act, gp, act_t, gp_t, in_sem,
     out_sem) = refs[21:]
    core = lax.axis_index("c")
    rows = refs[0].shape[0]
    hidden = wi_s.shape[0]
    half = w_own.shape[2]
    width = 2 * half
    feats = chunks * width

    def cols(z):
        return pl.ds(pl.multiple_of(z * width, width), width)

    def w_cols(z, which):
        return pl.ds(pl.multiple_of(z * width + which * half, half), half)

    def fetch(z, carry):
        for i, pair in enumerate(acts):
            at = pl.ds(i * rows, rows)
            for k, (source, buf) in enumerate(zip(pair, (p_s, g_s))):
                pltpu.make_async_copy(
                    source.at[:, cols(z)], buf.at[at, cols(z)], in_sem.at[k, z]
                ).start()
        for source, which in ((w_own, core), (w_oth, 1 - core)):
            pltpu.make_async_copy(
                source.at[z, pl.ds(0, hidden), :], wi_s.at[:, w_cols(z, which)], in_sem.at[2, z]
            ).start()
            pltpu.make_async_copy(
                source.at[z, pl.ds(hidden, hidden), :],
                wo_s.at[:, w_cols(z, which)],
                in_sem.at[3, z],
            ).start()
        return carry

    lax.fori_loop(0, chunks, fetch, 0)
    h_s[...] = jnp.zeros_like(h_s)
    ga_s[...] = jnp.zeros_like(ga_s)
    sq_s[...] = jnp.zeros_like(sq_s)

    def first(z, carry):
        for k, buf in enumerate((p_s, g_s, wi_s, wo_s)):
            view = buf.at[:, cols(z)]
            pltpu.make_async_copy(view, view, in_sem.at[k, z]).wait()
        p = p_s[:, cols(z)]
        h_s[...] += nt(p, wi_s[:, cols(z)])
        ga_s[...] += nt(g_s[:, cols(z)], wo_s[:, cols(z)])
        pf = p.astype(jnp.float32)
        sq_s[...] += jnp.sum(pf * pf, axis=1, keepdims=True)
        return carry

    lax.fori_loop(0, chunks, first, 0)
    inv = lax.rsqrt(sq_s[...] * (1.0 / feats) + 1e-05)
    v = h_s[...] * inv
    v2 = v * v
    t = jnp.tanh(0.7978845608 * v * (1.0 + 0.044715 * v2))
    up = 0.5 * (1.0 + t)
    a = (v * up).astype(jnp.bfloat16)
    slope = up + 0.5 * v * (1.0 - t * t) * (0.7978845608 * (1.0 + 0.134145 * v2))
    b = (ga_s[...] * slope * inv).astype(jnp.bfloat16)
    act[...] = a
    gp[...] = b
    act_t[...] = a.T
    gp_t[...] = b.T

    def second(z, carry):
        wi = wi_s[:, cols(z)]
        d_s[:, cols(z)] = nn(act[...], wo_s[:, cols(z)]).astype(jnp.bfloat16)
        n_s[:, cols(z)] = nn(gp[...], wi).astype(jnp.bfloat16)
        go_s[:, cols(z)] = nn(act_t[...], g_s[:, cols(z)]).astype(jnp.bfloat16)
        gi = nn(gp_t[...], p_s[:, cols(z)])
        gi_s[:, cols(z)] = gi.astype(jnp.bfloat16)
        gain[:, cols(z)] = jnp.sum(gi * wi.astype(jnp.float32), axis=0, keepdims=True)
        for i, pair in enumerate(outs):
            at = pl.ds(i * rows, rows)
            for k, (dest, buf) in enumerate(zip(pair, (d_s, n_s))):
                pltpu.make_async_copy(
                    buf.at[at, cols(z)], dest.at[:, cols(z)], out_sem.at[k, z]
                ).start()
        for dest, which in ((g_own, core), (g_oth, 1 - core)):
            pltpu.make_async_copy(
                gi_s.at[:, w_cols(z, which)], dest.at[z, pl.ds(0, hidden), :], out_sem.at[2, z]
            ).start()
            pltpu.make_async_copy(
                go_s.at[:, w_cols(z, which)], dest.at[z, pl.ds(hidden, hidden), :], out_sem.at[3, z]
            ).start()
        return carry

    lax.fori_loop(0, chunks, second, 0)

    def drain(z, carry):
        for k, buf in enumerate((d_s, n_s, gi_s, go_s)):
            view = buf.at[:, cols(z)]
            pltpu.make_async_copy(view, view, out_sem.at[k, z]).wait()
        return carry

    lax.fori_loop(0, chunks, drain, 0)


def block(acts, w_own, w_oth):
    rows, feats = acts[0].shape
    chunks, hidden2, half = w_own.shape
    hidden = hidden2 // 2
    total = 4 * rows
    bf = jnp.bfloat16
    anywhere = pl.BlockSpec(memory_space=pl.ANY)
    flops = 12 * total * feats * hidden
    return pl.pallas_call(
        functools.partial(block_kernel, chunks),
        out_shape=[jax.ShapeDtypeStruct(act.shape, bf) for act in acts]
        + [jax.ShapeDtypeStruct(w_own.shape, bf)] * 2
        + [jax.ShapeDtypeStruct((1, feats), jnp.float32)],
        in_specs=[anywhere] * 10,
        out_specs=[anywhere] * 10 + [pl.BlockSpec(memory_space=pltpu.VMEM)],
        scratch_shapes=[pltpu.VMEM((total, feats), bf)] * 2
        + [pltpu.VMEM((hidden, feats), bf)] * 2
        + [pltpu.VMEM((total, feats), bf)] * 2
        + [pltpu.VMEM((hidden, feats), bf)] * 2
        + [pltpu.VMEM((total, hidden), jnp.float32)] * 2
        + [pltpu.VMEM((total, 1), jnp.float32)]
        + [pltpu.VMEM((total, hidden), bf)] * 2
        + [pltpu.VMEM((hidden, total), bf)] * 2
        + [pltpu.SemaphoreType.DMA((4, chunks)), pltpu.SemaphoreType.DMA((4, chunks))],
        compiler_params=pltpu.CompilerParams(vmem_limit_bytes=48 * 1024 * 1024),
        cost_estimate=pl.CostEstimate(
            flops=flops, bytes_accessed=8 * (total + hidden) * feats * 2, transcendentals=0
        ),
    )(*acts, w_own, w_oth)


def add_all(parts):
    total = parts[0].astype(jnp.float32)
    for part in parts[1:]:
        total = total + part.astype(jnp.float32)
    return total


def gather_plane(acts):
    parts = [acts] + [shift(acts, first=d) for d in (1, 2, 3)]
    p0 = jnp.concatenate([part[0] for part in parts], axis=0)
    g0 = jnp.concatenate([part[1] for part in parts], axis=0)
    p0, g0 = lax.optimization_barrier((p0, g0))
    p1, g3 = shift(p0, second=1), shift(g0, second=-1)
    g1, p3 = shift(g0, second=1), shift(p0, second=-1)
    p1, g3, g1, p3 = lax.optimization_barrier((p1, g3, g1, p3))
    p2, g2 = shift(p1, second=1), shift(g3, second=-1)
    return [p0, p1, p2, p3, g0, g1, g2, g3]


def scatter_plane(outs, gain_part, weight_part):
    d0, d1, d2, d3, n0, n1, n2, n3 = outs
    bf = jnp.bfloat16
    d2, n2 = shift(d2, second=-1), shift(n2, second=1)
    n1, d3 = shift(n1, second=-1), shift(d3, second=1)
    d1, n3 = add_all([d1, d2]).astype(bf), add_all([n3, n2]).astype(bf)
    d1, n3, weight_part = lax.optimization_barrier((d1, n3, weight_part))
    weight_sum = lax.psum_scatter(weight_part, "z", scatter_dimension=0, tiled=False)
    d1, n3 = shift(d1, second=-1), shift(n3, second=1)
    arrived = (d1, d3, n1, n3, total_over_all(gain_part))
    d1, d3, n1, n3, grad_gain = lax.optimization_barrier(arrived)
    both = jnp.stack([add_all([d0, d1, d3]).astype(bf), add_all([n0, n1, n3]).astype(bf)])
    rows = both.shape[1] // 4
    both = [both[:, d * rows : (d + 1) * rows] for d in range(4)]
    arrived = [shift(both[d], first=-d) for d in (1, 2, 3)] + [weight_sum]
    *arrived, weight_sum = lax.optimization_barrier(arrived)
    return add_all([both[0], *arrived]), grad_gain, weight_sum


def total_over_all(value):
    moves = [lambda p, k=k: (p[0] ^ k, p[1], p[2], p[3]) for k in (1, 2, 4)]
    moves += [lambda p: (p[0], p[1], p[2], 1 - p[3])]
    moves += [lambda p, k=k: (p[0], p[1] ^ k, p[2], p[3]) for k in (1, 2)]
    moves += [lambda p, k=k: (p[0], p[1], p[2] ^ k, p[3]) for k in (1, 2)]
    for move in moves:
        value = value + lax.ppermute(
            value, AXES, [(linear(*p), linear(*move(p))) for p in places()]
        )
    return value


def shards(stream, doc_start, norm_gain, weight_in, weight_out, upstream):
    tok_rows, feats = stream.shape
    groups = tok_rows // 4
    hidden = weight_out.shape[0]
    k_rows = weight_in.shape[0]
    bf = jnp.bfloat16
    seq = lax.axis_index("z") * 2 + lax.axis_index("yl")
    gain = lax.dynamic_slice(norm_gain, (seq * k_rows,), (k_rows,))

    scaled_in = (weight_in.T.astype(jnp.float32) * gain[None, :]).astype(bf)
    both = swap_low(jnp.concatenate([scaled_in, weight_out], axis=0))
    w_own = lax.all_gather(both, "z", axis=0, tiled=False)

    starts = doc_start.reshape(groups, 4).astype(jnp.float32)
    keep = jnp.cumprod(1.0 - starts, axis=1).reshape(tok_rows)
    group_of = lax.broadcasted_iota(jnp.int32, (groups, tok_rows), 1) // 4
    here = lax.broadcasted_iota(jnp.int32, (groups, tok_rows), 0)
    pool = jnp.where(group_of == here, 0.25, 0.0).astype(bf)
    pooled = nn(pool, stream).astype(bf)
    pick = jnp.where(group_of == here, keep[None, :], 0.0).astype(bf)
    group_sums = nn(pick, upstream).astype(bf)
    following = from_behind(group_sums[:1], -1)
    grad_coarse = jnp.concatenate([group_sums[1:], following], axis=0)

    acts = jnp.stack([pooled, grad_coarse], axis=0)
    blocks = gather_plane(acts)
    w_own = lax.optimization_barrier((w_own, blocks[1], blocks[3]))[0]
    w_oth = other_core(w_own)
    results = block(blocks, w_own, w_oth)
    outs, (g_own, g_oth, gain_part) = results[:8], results[8:]

    mine = (g_own.astype(jnp.float32) + other_core(g_oth).astype(jnp.float32)).astype(bf)
    (down_sum, scaled), grad_gain, grads = scatter_plane(outs, gain_part[0] / norm_gain, mine)
    grads = swap_low(grads)
    grad_weight_in = (grads[:hidden].astype(jnp.float32) * gain[None, :]).T
    grad_weight_out = grads[hidden:].astype(jnp.float32)
    pooled_f = pooled.astype(jnp.float32)
    inv_sq = 1.0 / (jnp.mean(pooled_f * pooled_f, axis=1, keepdims=True) + 1e-05)
    coarse = (pooled_f + down_sum).astype(bf)
    carried = from_behind(coarse[groups - 1 :], 1)
    earlier = jnp.concatenate([carried, coarse[:-1]], axis=0)
    mixed_stream = (stream.astype(jnp.float32) + nn(pick.T, earlier)).astype(bf)
    grad_pooled = grad_coarse.astype(jnp.float32) + (
        scaled - pooled_f * inv_sq * jnp.mean(scaled * pooled_f, axis=1, keepdims=True)
    )
    grad_stream = (upstream.astype(jnp.float32) + nn(pool.T, grad_pooled.astype(bf))).astype(bf)
    return (mixed_stream, grad_stream, grad_gain, grad_weight_in, grad_weight_out)


def solution(mesh):
    fine = Mesh(mesh.devices.reshape(NZ, 2, NX, 2, 2), AXES)
    rows = P(AXES, None)
    seq, mp = ("z", "yl"), ("x", "yh", "c")
    in_specs = (rows, P(AXES), P(), P(seq, mp), P(mp, seq), rows)
    out_specs = (rows, rows, P(), P(seq, mp), P(mp, seq))
    return jax.shard_map(shards, mesh=fine, in_specs=in_specs, out_specs=out_specs, check_vma=False)
```

```python
import functools

import jax
import jax.numpy as jnp
from jax import lax
from jax.experimental import pallas as pl
from jax.experimental.pallas import tpu as pltpu
from jax.sharding import Mesh, PartitionSpec as P

AXES = ("z", "yl", "x", "yh", "c")
NZ, NY, NX = 8, 4, 4


def linear(z, y, x, c):
    return (((z * 2 + y % 2) * NX + x) * 2 + y // 2) * 2 + c


def places():
    return [
        (z, y, x, c) for z in range(NZ) for y in range(NY) for x in range(NX) for c in range(2)
    ]


def shift(value, first=0, second=0):
    pairs = []
    for z, y, x, c in places():
        dy, dx = (second, first) if c else (first, second)
        pairs.append((linear(z, y, x, c), linear(z, (y + dy) % NY, (x + dx) % NX, c)))
    return lax.ppermute(value, AXES, pairs)


def other_core(value):
    pairs = [(linear(z, y, x, c), linear(z, y, x, 1 - c)) for z, y, x, c in places()]
    return lax.ppermute(value, AXES, pairs)


def swap_low(value):
    pairs = [
        (linear(z, y, x, c), linear(z, (y // 2) * 2 + c, x, y % 2)) for z, y, x, c in places()
    ]
    return lax.ppermute(value, AXES, pairs)


def from_behind(value, by):
    count = NZ * NY * NX * 2
    pairs = [(i, i + by) for i in range(count) if 0 <= i + by < count]
    return lax.ppermute(value, AXES, pairs)


def nt(a, b):
    return lax.dot_general(a, b, (((1,), (1,)), ((), ())), preferred_element_type=jnp.float32)


def nn(a, b):
    return jnp.dot(a, b, preferred_element_type=jnp.float32)


def block_kernel(chunks, blocks, kept, *refs):
    refs = list(refs)

    def take(count):
        part = refs[:count]
        del refs[:count]
        return part

    last = kept > 0
    acts = list(zip(take(blocks), take(blocks)))
    olds = list(zip(take(kept), take(kept)))
    w_own, w_oth = take(2)
    old_act, old_gp = take(2) if last else (None, None)
    outs = list(zip(take(blocks), take(blocks)))
    if last:
        g_own, g_oth, gain = take(3)
    else:
        new_act, new_gp = take(2)
    p_s, g_s, wi_s, wo_s, d_s, n_s, h_s, ga_s, sq_s, act, gp, in_sem, out_sem = take(13)
    if last:
        gi_s, go_s, act_t, gp_t, old_sem = take(5)
    core = lax.axis_index("c")
    rows = acts[0][0].shape[0]
    fresh = rows * blocks
    hidden = wi_s.shape[0]
    half = w_own.shape[2]
    width = 2 * half
    feats = chunks * width

    def cols(z):
        return pl.ds(pl.multiple_of(z * width, width), width)

    def w_cols(z, which):
        return pl.ds(pl.multiple_of(z * width + which * half, half), half)

    def fetch(z, carry):
        for i, pair in enumerate(acts):
            at = pl.ds(i * rows, rows)
            for k, (source, buf) in enumerate(zip(pair, (p_s, g_s))):
                pltpu.make_async_copy(
                    source.at[:, cols(z)], buf.at[at, cols(z)], in_sem.at[k, z]
                ).start()
        for source, which in ((w_own, core), (w_oth, 1 - core)):
            pltpu.make_async_copy(
                source.at[z, pl.ds(0, hidden), :], wi_s.at[:, w_cols(z, which)], in_sem.at[2, z]
            ).start()
            pltpu.make_async_copy(
                source.at[z, pl.ds(hidden, hidden), :],
                wo_s.at[:, w_cols(z, which)],
                in_sem.at[3, z],
            ).start()
        return carry

    def fetch_old(z, carry):
        for i, pair in enumerate(olds):
            at = pl.ds(fresh + i * rows, rows)
            for k, (source, buf) in enumerate(zip(pair, (p_s, g_s))):
                pltpu.make_async_copy(
                    source.at[:, cols(z)], buf.at[at, cols(z)], old_sem.at[k, z]
                ).start()
        return carry

    lax.fori_loop(0, chunks, fetch, 0)
    if last:
        lax.fori_loop(0, chunks, fetch_old, 0)
    h_s[...] = jnp.zeros_like(h_s)
    ga_s[...] = jnp.zeros_like(ga_s)
    sq_s[...] = jnp.zeros_like(sq_s)

    def first(z, carry):
        for k, buf in enumerate((p_s.at[pl.ds(0, fresh)], g_s.at[pl.ds(0, fresh)], wi_s, wo_s)):
            view = buf.at[:, cols(z)]
            pltpu.make_async_copy(view, view, in_sem.at[k, z]).wait()
        p = p_s[pl.ds(0, fresh), cols(z)]
        h_s[...] += nt(p, wi_s[:, cols(z)])
        ga_s[...] += nt(g_s[pl.ds(0, fresh), cols(z)], wo_s[:, cols(z)])
        pf = p.astype(jnp.float32)
        sq_s[...] += jnp.sum(pf * pf, axis=1, keepdims=True)
        return carry

    lax.fori_loop(0, chunks, first, 0)
    inv = lax.rsqrt(sq_s[...] * (1.0 / feats) + 1e-05)
    v = h_s[...] * inv
    v2 = v * v
    t = jnp.tanh(0.7978845608 * v * (1.0 + 0.044715 * v2))
    up = 0.5 * (1.0 + t)
    a = (v * up).astype(jnp.bfloat16)
    slope = up + 0.5 * v * (1.0 - t * t) * (0.7978845608 * (1.0 + 0.134145 * v2))
    b = (ga_s[...] * slope * inv).astype(jnp.bfloat16)
    act[...] = a
    gp[...] = b
    if last:
        act_t[:, pl.ds(0, fresh)] = a.T
        gp_t[:, pl.ds(0, fresh)] = b.T
        act_t[:, pl.ds(fresh, rows * kept)] = old_act[...].T
        gp_t[:, pl.ds(fresh, rows * kept)] = old_gp[...].T
    else:
        new_act[...] = a
        new_gp[...] = b

    def second(z, carry):
        wi = wi_s[:, cols(z)]
        d_s[:, cols(z)] = nn(act[...], wo_s[:, cols(z)]).astype(jnp.bfloat16)
        n_s[:, cols(z)] = nn(gp[...], wi).astype(jnp.bfloat16)
        for i, pair in enumerate(outs):
            at = pl.ds(i * rows, rows)
            for k, (dest, buf) in enumerate(zip(pair, (d_s, n_s))):
                pltpu.make_async_copy(
                    buf.at[at, cols(z)], dest.at[:, cols(z)], out_sem.at[k, z]
                ).start()
        if not last:
            return carry
        for k, buf in enumerate((p_s, g_s)):
            view = buf.at[pl.ds(fresh, rows * kept), cols(z)]
            pltpu.make_async_copy(view, view, old_sem.at[k, z]).wait()
        go_s[:, cols(z)] = nn(act_t[...], g_s[:, cols(z)]).astype(jnp.bfloat16)
        gi = nn(gp_t[...], p_s[:, cols(z)])
        gi_s[:, cols(z)] = gi.astype(jnp.bfloat16)
        gain[:, cols(z)] = jnp.sum(gi * wi.astype(jnp.float32), axis=0, keepdims=True)
        for dest, which in ((g_own, core), (g_oth, 1 - core)):
            pltpu.make_async_copy(
                gi_s.at[:, w_cols(z, which)], dest.at[z, pl.ds(0, hidden), :], out_sem.at[2, z]
            ).start()
            pltpu.make_async_copy(
                go_s.at[:, w_cols(z, which)], dest.at[z, pl.ds(hidden, hidden), :], out_sem.at[3, z]
            ).start()
        return carry

    lax.fori_loop(0, chunks, second, 0)

    def drain(z, carry):
        for k, buf in enumerate((d_s, n_s, gi_s, go_s) if last else (d_s, n_s)):
            view = buf.at[:, cols(z)]
            pltpu.make_async_copy(view, view, out_sem.at[k, z]).wait()
        return carry

    lax.fori_loop(0, chunks, drain, 0)


def block(pooled, cotangent, w_own, w_oth, old=None):
    n = len(pooled)
    rows, feats = pooled[0].shape
    chunks, hidden2, half = w_own.shape
    hidden = hidden2 // 2
    bf = jnp.bfloat16
    old_p, old_g, old_acts = old or ([], [], [])
    kept = len(old_p)
    fresh, total = n * rows, (n + kept) * rows
    anywhere, inside = pl.BlockSpec(memory_space=pl.ANY), pl.BlockSpec(memory_space=pltpu.VMEM)
    out_shape = [jax.ShapeDtypeStruct((rows, feats), bf)] * (2 * n)
    out_specs = [anywhere] * (2 * n)
    scratch = [pltpu.VMEM((total, feats), bf)] * 2
    scratch += [pltpu.VMEM((hidden, feats), bf)] * 2
    scratch += [pltpu.VMEM((fresh, feats), bf)] * 2
    scratch += [pltpu.VMEM((fresh, hidden), jnp.float32)] * 2
    scratch += [pltpu.VMEM((fresh, 1), jnp.float32)]
    scratch += [pltpu.VMEM((fresh, hidden), bf)] * 2
    scratch += [pltpu.SemaphoreType.DMA((4, chunks))] * 2
    if kept:
        out_shape += [jax.ShapeDtypeStruct(w_own.shape, bf)] * 2
        out_shape += [jax.ShapeDtypeStruct((1, feats), jnp.float32)]
        out_specs += [anywhere, anywhere, inside]
        scratch += [pltpu.VMEM((hidden, feats), bf)] * 2
        scratch += [pltpu.VMEM((hidden, total), bf)] * 2
        scratch += [pltpu.SemaphoreType.DMA((2, chunks))]
    else:
        out_shape += [jax.ShapeDtypeStruct((fresh, hidden), bf)] * 2
        out_specs += [inside, inside]
    products = 4 * fresh + (2 * total if kept else 0)
    return pl.pallas_call(
        functools.partial(block_kernel, chunks, n, kept),
        out_shape=out_shape,
        in_specs=[anywhere] * (2 * n + 2 * kept + 2) + [inside] * len(old_acts),
        out_specs=out_specs,
        scratch_shapes=scratch,
        compiler_params=pltpu.CompilerParams(vmem_limit_bytes=48 * 1024 * 1024),
        cost_estimate=pl.CostEstimate(
            flops=2 * products * feats * hidden,
            bytes_accessed=2 * feats * (2 * total + 2 * fresh + (4 if kept else 2) * hidden),
            transcendentals=0,
        ),
    )(*pooled, *cotangent, *old_p, *old_g, w_own, w_oth, *old_acts)


def add_all(parts):
    total = parts[0].astype(jnp.float32)
    for part in parts[1:]:
        total = total + part.astype(jnp.float32)
    return total


def gather_plane(acts):
    parts = [acts] + [shift(acts, first=d) for d in (1, 2, 3)]
    p0 = jnp.concatenate([part[0] for part in parts], axis=0)
    g0 = jnp.concatenate([part[1] for part in parts], axis=0)
    p0, g0 = lax.optimization_barrier((p0, g0))
    p1, g3 = shift(p0, second=1), shift(g0, second=-1)
    g1, p3 = shift(g0, second=1), shift(p0, second=-1)
    p1, g3, g1, p3 = lax.optimization_barrier((p1, g3, g1, p3))
    p2, g2 = shift(p1, second=1), shift(g3, second=-1)
    return [p0, p1, p2, p3], [g0, g1, g2, g3]


def swapped(value, moves):
    for move in moves:
        value = value + lax.ppermute(
            value, AXES, [(linear(*p), linear(*move(p))) for p in places()]
        )
    return value


def all_moves():
    moves = [lambda p, k=k: (p[0] ^ k, p[1], p[2], p[3]) for k in (1, 2, 4)]
    moves += [lambda p: (p[0], p[1], p[2], 1 - p[3])]
    moves += [lambda p, k=k: (p[0], p[1] ^ k, p[2], p[3]) for k in (1, 2)]
    return moves + [lambda p, k=k: (p[0], p[1], p[2] ^ k, p[3]) for k in (1, 2)]


def scatter_plane(d0, d1, d2, d3, n0, n1, n2, n3, g_own, g_oth, gain):
    bf = jnp.bfloat16
    tie = lax.optimization_barrier
    moves = all_moves()
    n1, d3 = shift(n1, second=-1), shift(d3, second=1)
    mine = add_all([g_own, other_core(g_oth)]).astype(bf)
    weight_sum = lax.psum_scatter(mine, "z", scatter_dimension=0, tiled=False)
    d2, n2, n1, d3, gain = tie((d2, n2, n1, d3, swapped(gain, moves[:2])))
    d2, n2 = shift(d2, second=-1), shift(n2, second=1)
    gain = swapped(gain, moves[2:4])
    d1, n3 = add_all([d1, d2]).astype(bf), add_all([n3, n2]).astype(bf)
    d1, n3, gain = tie((d1, n3, gain))
    d1, n3, gain = tie((shift(d1, second=-1), shift(n3, second=1), swapped(gain, moves[4:6])))
    both = jnp.stack([add_all([d0, d1, d3]).astype(bf), add_all([n0, n1, n3]).astype(bf)])
    rows = both.shape[1] // 4
    both = [both[:, d * rows : (d + 1) * rows] for d in range(4)]
    arrived = [shift(both[d], first=-d) for d in (1, 2, 3)] + [weight_sum]
    gain = swapped(gain, moves[6:])
    *arrived, weight_sum, gain = tie((*arrived, gain))
    return add_all([both[0], *arrived]), gain, weight_sum


def shards(stream, doc_start, norm_gain, weight_in, weight_out, upstream):
    tok_rows, feats = stream.shape
    groups = tok_rows // 4
    hidden = weight_out.shape[0]
    k_rows = weight_in.shape[0]
    bf = jnp.bfloat16
    seq = lax.axis_index("z") * 2 + lax.axis_index("yl")
    gain = lax.dynamic_slice(norm_gain, (seq * k_rows,), (k_rows,))

    scaled_in = (weight_in.T.astype(jnp.float32) * gain[None, :]).astype(bf)
    both = swap_low(jnp.concatenate([scaled_in, weight_out], axis=0))
    w_own = lax.all_gather(both, "z", axis=0, tiled=False)

    starts = doc_start.reshape(groups, 4).astype(jnp.float32)
    keep = jnp.cumprod(1.0 - starts, axis=1).reshape(tok_rows)
    group_of = lax.broadcasted_iota(jnp.int32, (groups, tok_rows), 1) // 4
    here = lax.broadcasted_iota(jnp.int32, (groups, tok_rows), 0)
    pool = jnp.where(group_of == here, 0.25, 0.0).astype(bf)
    pooled = nn(pool, stream).astype(bf)
    pick = jnp.where(group_of == here, keep[None, :], 0.0).astype(bf)
    group_sums = nn(pick, upstream).astype(bf)
    following = from_behind(group_sums[:1], -1)
    grad_coarse = jnp.concatenate([group_sums[1:], following], axis=0)

    acts = jnp.stack([pooled, grad_coarse], axis=0)
    p, g = gather_plane(acts)
    w_own = lax.optimization_barrier((w_own, p[1], p[3]))[0]
    w_oth = other_core(w_own)
    early = [[part[0], part[1], part[3]] for part in (p, g)]
    d0, d1, d3, n0, n1, n3, *kept = block(*early, w_own, w_oth)
    d2, n2, g_own, g_oth, gain_part = block(p[2:3], g[2:3], w_own, w_oth, (*early, kept))
    (down_sum, scaled), grad_gain, grads = scatter_plane(
        d0, d1, d2, d3, n0, n1, n2, n3, g_own, g_oth, gain_part[0] / norm_gain
    )
    grads = swap_low(grads)
    grad_weight_in = (grads[:hidden].astype(jnp.float32) * gain[None, :]).T
    grad_weight_out = grads[hidden:].astype(jnp.float32)
    pooled_f = pooled.astype(jnp.float32)
    inv_sq = 1.0 / (jnp.mean(pooled_f * pooled_f, axis=1, keepdims=True) + 1e-05)
    coarse = (pooled_f + down_sum).astype(bf)
    carried = from_behind(coarse[groups - 1 :], 1)
    earlier = jnp.concatenate([carried, coarse[:-1]], axis=0)
    mixed_stream = (stream.astype(jnp.float32) + nn(pick.T, earlier)).astype(bf)
    grad_pooled = grad_coarse.astype(jnp.float32) + (
        scaled - pooled_f * inv_sq * jnp.mean(scaled * pooled_f, axis=1, keepdims=True)
    )
    grad_stream = (upstream.astype(jnp.float32) + nn(pool.T, grad_pooled.astype(bf))).astype(bf)
    return (mixed_stream, grad_stream, grad_gain, grad_weight_in, grad_weight_out)


def solution(mesh):
    fine = Mesh(mesh.devices.reshape(NZ, 2, NX, 2, 2), AXES)
    rows = P(AXES, None)
    seq, mp = ("z", "yl"), ("x", "yh", "c")
    in_specs = (rows, P(AXES), P(), P(seq, mp), P(mp, seq), rows)
    out_specs = (rows, rows, P(), P(seq, mp), P(mp, seq))
    return jax.shard_map(shards, mesh=fine, in_specs=in_specs, out_specs=out_specs, check_vma=False)
```

```python
import functools

import jax
import jax.numpy as jnp
from jax import lax
from jax.experimental import pallas as pl
from jax.experimental.pallas import tpu as pltpu
from jax.sharding import Mesh, PartitionSpec as P

AXES = ("z", "yl", "x", "yh", "c")
NZ, NY, NX = 8, 4, 4


def linear(z, y, x, c):
    return (((z * 2 + y % 2) * NX + x) * 2 + y // 2) * 2 + c


def places():
    return [
        (z, y, x, c) for z in range(NZ) for y in range(NY) for x in range(NX) for c in range(2)
    ]


def shift(value, first=0, second=0):
    pairs = []
    for z, y, x, c in places():
        dy, dx = (second, first) if c else (first, second)
        pairs.append((linear(z, y, x, c), linear(z, (y + dy) % NY, (x + dx) % NX, c)))
    return lax.ppermute(value, AXES, pairs)


def other_core(value):
    pairs = [(linear(z, y, x, c), linear(z, y, x, 1 - c)) for z, y, x, c in places()]
    return lax.ppermute(value, AXES, pairs)


def swap_low(value):
    pairs = [
        (linear(z, y, x, c), linear(z, (y // 2) * 2 + c, x, y % 2)) for z, y, x, c in places()
    ]
    return lax.ppermute(value, AXES, pairs)


def from_behind(value, by):
    count = NZ * NY * NX * 2
    pairs = [(i, i + by) for i in range(count) if 0 <= i + by < count]
    return lax.ppermute(value, AXES, pairs)


def nt(a, b):
    return lax.dot_general(a, b, (((1,), (1,)), ((), ())), preferred_element_type=jnp.float32)


def nn(a, b):
    return jnp.dot(a, b, preferred_element_type=jnp.float32)


def pieces(refs):
    o0, o1, o3, o2p, o2g = refs[:5]
    own = [(o0.at[0], o0.at[1]), (o1.at[0], o1.at[1]), (o2p, o2g), (o3.at[0], o3.at[1])]
    return own + list(zip(refs[5:9], refs[9:13]))


def spans(pairs):
    start = 0
    for pair in pairs:
        rows = pair[0].shape[0]
        yield pl.ds(start, rows), pair
        start += rows


def block_kernel(chunks, *refs):
    acts, outs = pieces(refs[:13]), pieces(refs[16:29])
    w_own, w_oth, rgain = refs[13:16]
    g_own, g_oth, gain = refs[29:32]
    (p_s, g_s, wi_s, wo_s, d_s, n_s, gi_s, go_s, h_s, ga_s, sq_s, act, gp, act_t, gp_t, in_sem,
     out_sem) = refs[32:]
    core = lax.axis_index("c")
    hidden = wi_s.shape[0]
    half = w_own.shape[2]
    width = 2 * half
    feats = chunks * width

    def cols(z):
        return pl.ds(pl.multiple_of(z * width, width), width)

    def w_cols(z, which):
        return pl.ds(pl.multiple_of(z * width + which * half, half), half)

    def fetch(z, carry):
        for at, pair in spans(acts):
            for k, (source, buf) in enumerate(zip(pair, (p_s, g_s))):
                pltpu.make_async_copy(
                    source.at[:, cols(z)], buf.at[at, cols(z)], in_sem.at[k, z]
                ).start()
        for source, which in ((w_own, core), (w_oth, 1 - core)):
            pltpu.make_async_copy(
                source.at[z, pl.ds(0, hidden), :], wi_s.at[:, w_cols(z, which)], in_sem.at[2, z]
            ).start()
            pltpu.make_async_copy(
                source.at[z, pl.ds(hidden, hidden), :],
                wo_s.at[:, w_cols(z, which)],
                in_sem.at[3, z],
            ).start()
        return carry

    lax.fori_loop(0, chunks, fetch, 0)
    h_s[...] = jnp.zeros_like(h_s)
    ga_s[...] = jnp.zeros_like(ga_s)
    sq_s[...] = jnp.zeros_like(sq_s)

    def first(z, carry):
        for k, buf in enumerate((p_s, g_s, wi_s, wo_s)):
            view = buf.at[:, cols(z)]
            pltpu.make_async_copy(view, view, in_sem.at[k, z]).wait()
        p = p_s[:, cols(z)]
        h_s[...] += nt(p, wi_s[:, cols(z)])
        ga_s[...] += nt(g_s[:, cols(z)], wo_s[:, cols(z)])
        pf = p.astype(jnp.float32) * rgain[:, cols(z)]
        sq_s[...] += jnp.sum(pf * pf, axis=1, keepdims=True)
        return carry

    lax.fori_loop(0, chunks, first, 0)
    inv = lax.rsqrt(sq_s[...] * (1.0 / feats) + 1e-05)
    v = h_s[...] * inv
    v2 = v * v
    t = jnp.tanh(0.7978845608 * v * (1.0 + 0.044715 * v2))
    up = 0.5 * (1.0 + t)
    a = (v * up).astype(jnp.bfloat16)
    slope = up + 0.5 * v * (1.0 - t * t) * (0.7978845608 * (1.0 + 0.134145 * v2))
    b = (ga_s[...] * slope * inv).astype(jnp.bfloat16)
    act[...] = a
    gp[...] = b
    act_t[...] = a.T
    gp_t[...] = b.T

    def second(z, carry):
        wi = wi_s[:, cols(z)]
        d_s[:, cols(z)] = nn(act[...], wo_s[:, cols(z)]).astype(jnp.bfloat16)
        n_s[:, cols(z)] = nn(gp[...], wi).astype(jnp.bfloat16)
        go_s[:, cols(z)] = nn(act_t[...], g_s[:, cols(z)]).astype(jnp.bfloat16)
        gi = nn(gp_t[...], p_s[:, cols(z)])
        gi_s[:, cols(z)] = gi.astype(jnp.bfloat16)
        total = jnp.sum(gi * wi.astype(jnp.float32), axis=0, keepdims=True)
        gain[:, cols(z)] = total * rgain[:, cols(z)]
        for at, pair in spans(outs):
            for k, (dest, buf) in enumerate(zip(pair, (d_s, n_s))):
                pltpu.make_async_copy(
                    buf.at[at, cols(z)], dest.at[:, cols(z)], out_sem.at[k, z]
                ).start()
        for dest, which in ((g_own, core), (g_oth, 1 - core)):
            pltpu.make_async_copy(
                gi_s.at[:, w_cols(z, which)], dest.at[z, pl.ds(0, hidden), :], out_sem.at[2, z]
            ).start()
            pltpu.make_async_copy(
                go_s.at[:, w_cols(z, which)], dest.at[z, pl.ds(hidden, hidden), :], out_sem.at[3, z]
            ).start()
        return carry

    lax.fori_loop(0, chunks, second, 0)

    def drain(z, carry):
        for k, buf in enumerate((d_s, n_s, gi_s, go_s)):
            view = buf.at[:, cols(z)]
            pltpu.make_async_copy(view, view, out_sem.at[k, z]).wait()
        return carry

    lax.fori_loop(0, chunks, drain, 0)


def block(acts, w_own, w_oth, rgain):
    feats = acts[0].shape[-1]
    chunks, hidden2, half = w_own.shape
    hidden = hidden2 // 2
    total = 4 * (acts[0].shape[1] + acts[5].shape[0])
    bf = jnp.bfloat16
    anywhere, inside = pl.BlockSpec(memory_space=pl.ANY), pl.BlockSpec(memory_space=pltpu.VMEM)
    results = pl.pallas_call(
        functools.partial(block_kernel, chunks),
        out_shape=[jax.ShapeDtypeStruct(act.shape, bf) for act in acts]
        + [jax.ShapeDtypeStruct(w_own.shape, bf)] * 2
        + [jax.ShapeDtypeStruct((1, feats), jnp.float32)],
        in_specs=[anywhere] * 15 + [inside],
        out_specs=[anywhere] * 15 + [inside],
        scratch_shapes=[pltpu.VMEM((total, feats), bf)] * 2
        + [pltpu.VMEM((hidden, feats), bf)] * 2
        + [pltpu.VMEM((total, feats), bf)] * 2
        + [pltpu.VMEM((hidden, feats), bf)] * 2
        + [pltpu.VMEM((total, hidden), jnp.float32)] * 2
        + [pltpu.VMEM((total, 1), jnp.float32)]
        + [pltpu.VMEM((total, hidden), bf)] * 2
        + [pltpu.VMEM((hidden, total), bf)] * 2
        + [pltpu.SemaphoreType.DMA((4, chunks)), pltpu.SemaphoreType.DMA((4, chunks))],
        compiler_params=pltpu.CompilerParams(vmem_limit_bytes=48 * 1024 * 1024),
        cost_estimate=pl.CostEstimate(
            flops=12 * total * feats * hidden,
            bytes_accessed=8 * (total + hidden) * feats * 2,
            transcendentals=0,
        ),
    )(*acts, w_own, w_oth, rgain)
    return results[:13], results[13:]


def add_all(parts):
    total = parts[0].astype(jnp.float32)
    for part in parts[1:]:
        total = total + part.astype(jnp.float32)
    return total


def gather_plane(acts):
    tie = lax.optimization_barrier
    parts = [shift(acts, first=d) for d in (1, 2, 3)]
    o1, o3 = shift(acts, second=1), shift(acts, second=-1)
    p0 = jnp.concatenate([part[0] for part in parts], axis=0)
    g0 = jnp.concatenate([part[1] for part in parts], axis=0)
    p0, g0, o1, o3 = tie((p0, g0, o1, o3))
    p1, g3 = shift(p0, second=1), shift(g0, second=-1)
    g1, p3 = shift(g0, second=1), shift(p0, second=-1)
    o2p, o2g = shift(o1[0], second=1), shift(o3[1], second=-1)
    p1, g3, g1, p3, o2p, o2g = tie((p1, g3, g1, p3, o2p, o2g))
    p2, g2 = shift(p1, second=1), shift(g3, second=-1)
    return [acts, o1, o3, o2p, o2g, p0, p1, p2, p3, g0, g1, g2, g3]


def swapped(value, moves):
    for move in moves:
        value = value + lax.ppermute(
            value, AXES, [(linear(*p), linear(*move(p))) for p in places()]
        )
    return value


def all_moves():
    moves = [lambda p, k=k: (p[0] ^ k, p[1], p[2], p[3]) for k in (1, 2, 4)]
    moves += [lambda p: (p[0], p[1], p[2], 1 - p[3])]
    moves += [lambda p, k=k: (p[0], p[1] ^ k, p[2], p[3]) for k in (1, 2)]
    return moves + [lambda p, k=k: (p[0], p[1], p[2] ^ k, p[3]) for k in (1, 2)]


def rounded_sum(*parts):
    return add_all(parts).astype(jnp.bfloat16)


def scatter_plane(outs, g_own, g_oth, gain):
    o0, o1, o3, od2, on2, d0, d1, d2, d3, n0, n1, n2, n3 = outs
    tie = lax.optimization_barrier
    moves = all_moves()
    d2, n2 = shift(d2, second=-1), shift(n2, second=1)
    n1, d3 = shift(n1, second=-1), shift(d3, second=1)
    mine = rounded_sum(g_own, other_core(g_oth))
    weight_sum = lax.psum_scatter(mine, "z", scatter_dimension=0, tiled=False)
    d1, n3 = rounded_sum(d1, d2), rounded_sum(n3, n2)
    d1, n3, n1, d3, od2, on2, gain, _ = tie((d1, n3, n1, d3, od2, on2, gain, mine))
    od2, on2 = shift(od2, second=-1), shift(on2, second=1)
    d1, n3 = shift(d1, second=-1), shift(n3, second=1)
    o1 = jnp.stack([rounded_sum(o1[0], od2), o1[1]])
    o3 = jnp.stack([o3[0], rounded_sum(o3[1], on2)])
    both = jnp.stack([rounded_sum(d0, d1, d3), rounded_sum(n0, n1, n3)])
    both, o1, o3 = tie((both, o1, o3))
    rows = both.shape[1] // 3
    arrived = [shift(both[:, d * rows - rows : d * rows], first=-d) for d in (1, 2, 3)]
    gain, *ours = tie((gain, shift(o1, second=-1), shift(o3, second=1)))
    gain = swapped(gain, moves)
    *arrived, weight_sum = tie((*arrived, weight_sum))
    return add_all([o0, *arrived, *ours]), gain, weight_sum


def shards(stream, doc_start, norm_gain, weight_in, weight_out, upstream):
    tok_rows, feats = stream.shape
    groups = tok_rows // 4
    hidden = weight_out.shape[0]
    bf = jnp.bfloat16
    both = swap_low(jnp.concatenate([weight_in.T, weight_out], axis=0))
    w_own = lax.all_gather(both, "z", axis=0, tiled=False)

    starts = doc_start.reshape(groups, 4).astype(jnp.float32)
    keep = jnp.cumprod(1.0 - starts, axis=1).reshape(tok_rows)
    group_of = lax.broadcasted_iota(jnp.int32, (groups, tok_rows), 1) // 4
    here = lax.broadcasted_iota(jnp.int32, (groups, tok_rows), 0)
    pool = jnp.where(group_of == here, 0.25, 0.0).astype(bf)
    pooled = nn(pool, stream).astype(bf)
    pick = jnp.where(group_of == here, keep[None, :], 0.0).astype(bf)
    group_sums = nn(pick, upstream).astype(bf)
    following = from_behind(group_sums[:1], -1)
    grad_coarse = jnp.concatenate([group_sums[1:], following], axis=0)

    scaled = (pooled.astype(jnp.float32) * norm_gain[None, :]).astype(bf)
    acts = jnp.stack([scaled, grad_coarse], axis=0)
    blocks = gather_plane(acts)
    w_own = lax.optimization_barrier((w_own, blocks[6], blocks[8]))[0]
    w_oth = other_core(w_own)
    outs, (g_own, g_oth, gain_part) = block(blocks, w_own, w_oth, 1.0 / norm_gain[None, :])
    (down_sum, grad_normed), grad_gain, grads = scatter_plane(outs, g_own, g_oth, gain_part[0])
    grads = swap_low(grads)
    grad_weight_in = grads[:hidden].astype(jnp.float32).T
    grad_weight_out = grads[hidden:].astype(jnp.float32)

    scaled = norm_gain * grad_normed
    pooled_f = pooled.astype(jnp.float32)
    inv_sq = 1.0 / (jnp.mean(pooled_f * pooled_f, axis=1, keepdims=True) + 1e-05)
    coarse = (pooled_f + down_sum).astype(bf)
    carried = from_behind(coarse[groups - 1 :], 1)
    earlier = jnp.concatenate([carried, coarse[:-1]], axis=0)
    mixed_stream = (stream.astype(jnp.float32) + nn(pick.T, earlier)).astype(bf)
    grad_pooled = grad_coarse.astype(jnp.float32) + (
        scaled - pooled_f * inv_sq * jnp.mean(scaled * pooled_f, axis=1, keepdims=True)
    )
    grad_stream = (upstream.astype(jnp.float32) + nn(pool.T, grad_pooled.astype(bf))).astype(bf)
    return (mixed_stream, grad_stream, grad_gain, grad_weight_in, grad_weight_out)


def solution(mesh):
    fine = Mesh(mesh.devices.reshape(NZ, 2, NX, 2, 2), AXES)
    rows = P(AXES, None)
    seq, mp = ("z", "yl"), ("x", "yh", "c")
    in_specs = (rows, P(AXES), P(), P(seq, mp), P(mp, seq), rows)
    out_specs = (rows, rows, P(), P(seq, mp), P(mp, seq))
    return jax.shard_map(shards, mesh=fine, in_specs=in_specs, out_specs=out_specs, check_vma=False)
```

```python
import functools

import jax
import jax.numpy as jnp
from jax import lax
from jax.experimental import pallas as pl
from jax.experimental.pallas import tpu as pltpu
from jax.sharding import Mesh, PartitionSpec as P

AXES = ("z", "yl", "x", "yh", "c")
NZ, NY, NX = 8, 4, 4


def linear(z, y, x, c):
    return (((z * 2 + y % 2) * NX + x) * 2 + y // 2) * 2 + c


def places():
    return [
        (z, y, x, c) for z in range(NZ) for y in range(NY) for x in range(NX) for c in range(2)
    ]


def shift(value, first=0, second=0):
    pairs = []
    for z, y, x, c in places():
        dy, dx = (second, first) if c else (first, second)
        pairs.append((linear(z, y, x, c), linear(z, (y + dy) % NY, (x + dx) % NX, c)))
    return lax.ppermute(value, AXES, pairs)


def other_core(value):
    pairs = [(linear(z, y, x, c), linear(z, y, x, 1 - c)) for z, y, x, c in places()]
    return lax.ppermute(value, AXES, pairs)


def swap_low(value):
    pairs = [
        (linear(z, y, x, c), linear(z, (y // 2) * 2 + c, x, y % 2)) for z, y, x, c in places()
    ]
    return lax.ppermute(value, AXES, pairs)


def from_behind(value, by):
    count = NZ * NY * NX * 2
    pairs = [(i, i + by) for i in range(count) if 0 <= i + by < count]
    return lax.ppermute(value, AXES, pairs)


def nt(a, b):
    return lax.dot_general(a, b, (((1,), (1,)), ((), ())), preferred_element_type=jnp.float32)


def nn(a, b):
    return jnp.dot(a, b, preferred_element_type=jnp.float32)


def block_kernel(chunks, *refs):
    acts = list(zip(refs[:4], refs[4:8]))
    w_own, w_oth = refs[8:10]
    outs = list(zip(refs[10:14], refs[14:18]))
    g_own, g_oth, gain = refs[18:21]
    (p_s, g_s, wi_s, wo_s, d_s, n_s, gi_s, go_s, h_s, ga_s, sq_s, act, gp, act_t, gp_t, in_sem,
     out_sem) = refs[21:]
    core = lax.axis_index("c")
    rows = refs[0].shape[0]
    hidden = wi_s.shape[0]
    half = w_own.shape[2]
    width = 2 * half
    feats = chunks * width

    def cols(z):
        start = z * width
        return pl.ds(start if isinstance(z, int) else pl.multiple_of(start, width), width)

    def w_cols(z, which):
        return pl.ds(pl.multiple_of(z * width + which * half, half), half)

    def fetch(z):
        for i, pair in enumerate(acts):
            at = pl.ds(i * rows, rows)
            for k, (source, buf) in enumerate(zip(pair, (p_s, g_s))):
                pltpu.make_async_copy(
                    source.at[:, cols(z)], buf.at[at, cols(z)], in_sem.at[k, z]
                ).start()
        for source, which in ((w_own, core), (w_oth, 1 - core)):
            pltpu.make_async_copy(
                source.at[z, pl.ds(0, hidden), :], wi_s.at[:, w_cols(z, which)], in_sem.at[2, z]
            ).start()
            pltpu.make_async_copy(
                source.at[z, pl.ds(hidden, hidden), :],
                wo_s.at[:, w_cols(z, which)],
                in_sem.at[3, z],
            ).start()

    ahead = 3
    for z in range(ahead):
        fetch(z)
    h_s[...] = jnp.zeros_like(h_s)
    ga_s[...] = jnp.zeros_like(ga_s)
    sq_s[...] = jnp.zeros_like(sq_s)

    def first(z, carry):
        @pl.when(z + ahead < chunks)
        def _():
            fetch(z + ahead)

        for k, buf in enumerate((p_s, g_s, wi_s, wo_s)):
            view = buf.at[:, cols(z)]
            pltpu.make_async_copy(view, view, in_sem.at[k, z]).wait()
        p = p_s[:, cols(z)]
        h_s[...] += nt(p, wi_s[:, cols(z)])
        ga_s[...] += nt(g_s[:, cols(z)], wo_s[:, cols(z)])
        pf = p.astype(jnp.float32)
        sq_s[...] += jnp.sum(pf * pf, axis=1, keepdims=True)
        return carry

    lax.fori_loop(0, chunks, first, 0)

    def middle(i, carry):
        at = pl.ds(pl.multiple_of(i * 32, 32), 32)
        inv = lax.rsqrt(sq_s[at, :] * (1.0 / feats) + 1e-05)
        v = h_s[at, :] * inv
        v2 = v * v
        t = jnp.tanh(0.7978845608 * v * (1.0 + 0.044715 * v2))
        up = 0.5 * (1.0 + t)
        act[at, :] = (v * up).astype(jnp.bfloat16)
        slope = up + 0.5 * v * (1.0 - t * t) * (0.7978845608 * (1.0 + 0.134145 * v2))
        gp[at, :] = (ga_s[at, :] * slope * inv).astype(jnp.bfloat16)
        return carry

    lax.fori_loop(0, act.shape[0] // 32, middle, 0)
    act_t[...] = act[...].T
    gp_t[...] = gp[...].T

    def second(z, carry):
        wi = wi_s[:, cols(z)]
        d_s[:, cols(z)] = nn(act[...], wo_s[:, cols(z)]).astype(jnp.bfloat16)
        n_s[:, cols(z)] = nn(gp[...], wi).astype(jnp.bfloat16)
        go_s[:, cols(z)] = nn(act_t[...], g_s[:, cols(z)]).astype(jnp.bfloat16)
        gi = nn(gp_t[...], p_s[:, cols(z)])
        gi_s[:, cols(z)] = gi.astype(jnp.bfloat16)
        gain[:, cols(z)] = jnp.sum(gi * wi.astype(jnp.float32), axis=0, keepdims=True)
        for i, pair in enumerate(outs):
            at = pl.ds(i * rows, rows)
            for k, (dest, buf) in enumerate(zip(pair, (d_s, n_s))):
                pltpu.make_async_copy(
                    buf.at[at, cols(z)], dest.at[:, cols(z)], out_sem.at[k, z]
                ).start()
        for dest, which in ((g_own, core), (g_oth, 1 - core)):
            pltpu.make_async_copy(
                gi_s.at[:, w_cols(z, which)], dest.at[z, pl.ds(0, hidden), :], out_sem.at[2, z]
            ).start()
            pltpu.make_async_copy(
                go_s.at[:, w_cols(z, which)], dest.at[z, pl.ds(hidden, hidden), :], out_sem.at[3, z]
            ).start()
        return carry

    lax.fori_loop(0, chunks, second, 0)

    def drain(z, carry):
        for k, buf in enumerate((d_s, n_s, gi_s, go_s)):
            view = buf.at[:, cols(z)]
            pltpu.make_async_copy(view, view, out_sem.at[k, z]).wait()
        return carry

    lax.fori_loop(0, chunks, drain, 0)


def block(acts, w_own, w_oth):
    rows, feats = acts[0].shape
    chunks, hidden2, half = w_own.shape
    hidden = hidden2 // 2
    total = 4 * rows
    bf = jnp.bfloat16
    anywhere = pl.BlockSpec(memory_space=pl.ANY)
    flops = 12 * total * feats * hidden
    return pl.pallas_call(
        functools.partial(block_kernel, chunks),
        out_shape=[jax.ShapeDtypeStruct(act.shape, bf) for act in acts]
        + [jax.ShapeDtypeStruct(w_own.shape, bf)] * 2
        + [jax.ShapeDtypeStruct((1, feats), jnp.float32)],
        in_specs=[anywhere] * 10,
        out_specs=[anywhere] * 10 + [pl.BlockSpec(memory_space=pltpu.VMEM)],
        scratch_shapes=[pltpu.VMEM((total, feats), bf)] * 2
        + [pltpu.VMEM((hidden, feats), bf)] * 2
        + [pltpu.VMEM((total, feats), bf)] * 2
        + [pltpu.VMEM((hidden, feats), bf)] * 2
        + [pltpu.VMEM((total, hidden), jnp.float32)] * 2
        + [pltpu.VMEM((total, 1), jnp.float32)]
        + [pltpu.VMEM((total, hidden), bf)] * 2
        + [pltpu.VMEM((hidden, total), bf)] * 2
        + [pltpu.SemaphoreType.DMA((4, chunks)), pltpu.SemaphoreType.DMA((4, chunks))],
        compiler_params=pltpu.CompilerParams(vmem_limit_bytes=40 * 1024 * 1024),
        cost_estimate=pl.CostEstimate(
            flops=flops, bytes_accessed=8 * (total + hidden) * feats * 2, transcendentals=0
        ),
    )(*acts, w_own, w_oth)


def add_all(parts):
    total = parts[0].astype(jnp.float32)
    for part in parts[1:]:
        total = total + part.astype(jnp.float32)
    return total


def gather_plane(acts):
    parts = [acts] + [shift(acts, first=d) for d in (1, 2, 3)]
    p0 = jnp.concatenate([part[0] for part in parts], axis=0)
    g0 = jnp.concatenate([part[1] for part in parts], axis=0)
    p0, g0 = lax.optimization_barrier((p0, g0))
    p1, g3 = shift(p0, second=1), shift(g0, second=-1)
    g1, p3 = shift(g0, second=1), shift(p0, second=-1)
    p1, g3, g1, p3 = lax.optimization_barrier((p1, g3, g1, p3))
    p2, g2 = shift(p1, second=1), shift(g3, second=-1)
    return [p0, p1, p2, p3, g0, g1, g2, g3]


def swapped(value, moves):
    for move in moves:
        value = value + lax.ppermute(
            value, AXES, [(linear(*p), linear(*move(p))) for p in places()]
        )
    return value


def all_moves():
    moves = [lambda p, k=k: (p[0] ^ k, p[1], p[2], p[3]) for k in (1, 2, 4)]
    moves += [lambda p: (p[0], p[1], p[2], 1 - p[3])]
    moves += [lambda p, k=k: (p[0], p[1] ^ k, p[2], p[3]) for k in (1, 2)]
    return moves + [lambda p, k=k: (p[0], p[1], p[2] ^ k, p[3]) for k in (1, 2)]


def rounded_sum(*parts):
    return add_all(parts).astype(jnp.bfloat16)


def scatter_plane(outs, g_own, g_oth, gain):
    d0, d1, d2, d3, n0, n1, n2, n3 = outs
    tie = lax.optimization_barrier
    moves = all_moves()
    d2, n2 = shift(d2, second=-1), shift(n2, second=1)
    n1, d3 = shift(n1, second=-1), shift(d3, second=1)
    mine = rounded_sum(g_own, other_core(g_oth))
    weight_sum = lax.psum_scatter(mine, "z", scatter_dimension=0, tiled=False)
    d1, n3 = rounded_sum(d1, d2), rounded_sum(n3, n2)
    d1, n3, n1, d3, gain, _ = tie((d1, n3, n1, d3, gain, mine))
    d1, n3, gain = tie((shift(d1, second=-1), shift(n3, second=1), swapped(gain, moves[:3])))
    both = jnp.stack([rounded_sum(d0, d1, d3), rounded_sum(n0, n1, n3)])
    rows = both.shape[1] // 4
    both = [both[:, d * rows : (d + 1) * rows] for d in range(4)]
    arrived = [shift(both[d], first=-d) for d in (1, 2, 3)]
    *arrived, gain, weight_sum = tie((*arrived, swapped(gain, moves[3:6]), weight_sum))
    return add_all([both[0], *arrived]), swapped(gain, moves[6:]), weight_sum


def shards(stream, doc_start, norm_gain, weight_in, weight_out, upstream):
    tok_rows, feats = stream.shape
    groups = tok_rows // 4
    hidden = weight_out.shape[0]
    k_rows = weight_in.shape[0]
    bf = jnp.bfloat16
    seq = lax.axis_index("z") * 2 + lax.axis_index("yl")
    gain = lax.dynamic_slice(norm_gain, (seq * k_rows,), (k_rows,))

    scaled_in = (weight_in.T.astype(jnp.float32) * gain[None, :]).astype(bf)
    both = swap_low(jnp.concatenate([scaled_in, weight_out], axis=0))
    w_own = lax.all_gather(both, "z", axis=0, tiled=False)

    starts = doc_start.reshape(groups, 4).astype(jnp.float32)
    keep = jnp.cumprod(1.0 - starts, axis=1).reshape(tok_rows)
    group_of = lax.broadcasted_iota(jnp.int32, (groups, tok_rows), 1) // 4
    here = lax.broadcasted_iota(jnp.int32, (groups, tok_rows), 0)
    pool = jnp.where(group_of == here, 0.25, 0.0).astype(bf)
    pooled = nn(pool, stream).astype(bf)
    pick = jnp.where(group_of == here, keep[None, :], 0.0).astype(bf)
    group_sums = nn(pick, upstream).astype(bf)
    following = from_behind(group_sums[:1], -1)
    grad_coarse = jnp.concatenate([group_sums[1:], following], axis=0)

    acts = jnp.stack([pooled, grad_coarse], axis=0)
    blocks = gather_plane(acts)
    w_own = lax.optimization_barrier((w_own, blocks[1], blocks[3]))[0]
    w_oth = other_core(w_own)
    results = block(blocks, w_own, w_oth)
    outs, (g_own, g_oth, gain_part) = results[:8], results[8:]
    (down_sum, scaled), grad_gain, grads = scatter_plane(
        outs, g_own, g_oth, gain_part[0] / norm_gain
    )
    grads = swap_low(grads)
    grad_weight_in = (grads[:hidden].astype(jnp.float32) * gain[None, :]).T
    grad_weight_out = grads[hidden:].astype(jnp.float32)
    pooled_f = pooled.astype(jnp.float32)
    inv_sq = 1.0 / (jnp.mean(pooled_f * pooled_f, axis=1, keepdims=True) + 1e-05)
    coarse = (pooled_f + down_sum).astype(bf)
    carried = from_behind(coarse[groups - 1 :], 1)
    earlier = jnp.concatenate([carried, coarse[:-1]], axis=0)
    mixed_stream = (stream.astype(jnp.float32) + nn(pick.T, earlier)).astype(bf)
    grad_pooled = grad_coarse.astype(jnp.float32) + (
        scaled - pooled_f * inv_sq * jnp.mean(scaled * pooled_f, axis=1, keepdims=True)
    )
    grad_stream = (upstream.astype(jnp.float32) + nn(pool.T, grad_pooled.astype(bf))).astype(bf)
    return (mixed_stream, grad_stream, grad_gain, grad_weight_in, grad_weight_out)


def solution(mesh):
    fine = Mesh(mesh.devices.reshape(NZ, 2, NX, 2, 2), AXES)
    rows = P(AXES, None)
    seq, mp = ("z", "yl"), ("x", "yh", "c")
    in_specs = (rows, P(AXES), P(), P(seq, mp), P(mp, seq), rows)
    out_specs = (rows, rows, P(), P(seq, mp), P(mp, seq))
    return jax.shard_map(shards, mesh=fine, in_specs=in_specs, out_specs=out_specs, check_vma=False)
```

```python
import functools

import jax
import jax.numpy as jnp
from jax import lax
from jax.experimental import pallas as pl
from jax.experimental.pallas import tpu as pltpu
from jax.sharding import Mesh, PartitionSpec as P

AXES = ("z", "yl", "x", "yh", "c")
NZ, NY, NX = 8, 4, 4


def linear(z, y, x, c):
    return (((z * 2 + y % 2) * NX + x) * 2 + y // 2) * 2 + c


def places():
    return [
        (z, y, x, c) for z in range(NZ) for y in range(NY) for x in range(NX) for c in range(2)
    ]


def shift(value, first=0, second=0):
    pairs = []
    for z, y, x, c in places():
        dy, dx = (second, first) if c else (first, second)
        pairs.append((linear(z, y, x, c), linear(z, (y + dy) % NY, (x + dx) % NX, c)))
    return lax.ppermute(value, AXES, pairs)


def other_core(value):
    pairs = [(linear(z, y, x, c), linear(z, y, x, 1 - c)) for z, y, x, c in places()]
    return lax.ppermute(value, AXES, pairs)


def swap_low(value):
    pairs = [
        (linear(z, y, x, c), linear(z, (y // 2) * 2 + c, x, y % 2)) for z, y, x, c in places()
    ]
    return lax.ppermute(value, AXES, pairs)


def from_behind(value, by):
    count = NZ * NY * NX * 2
    pairs = [(i, i + by) for i in range(count) if 0 <= i + by < count]
    return lax.ppermute(value, AXES, pairs)


def nt(a, b):
    return lax.dot_general(a, b, (((1,), (1,)), ((), ())), preferred_element_type=jnp.float32)


def nn(a, b):
    return jnp.dot(a, b, preferred_element_type=jnp.float32)


def block_kernel(chunks, *refs):
    acts = list(zip(refs[:4], refs[4:8]))
    w_own, w_oth = refs[8:10]
    outs = list(zip(refs[10:14], refs[14:18]))
    g_own, g_oth, gain = refs[18:21]
    (p_s, g_s, wi_s, wo_s, d_s, n_s, gi_s, go_s, h_s, ga_s, sq_s, act, gp, act_t, gp_t, in_sem,
     out_sem) = refs[21:]
    core = lax.axis_index("c")
    rows = refs[0].shape[0]
    hidden = wi_s.shape[0]
    half = w_own.shape[2]
    width = 2 * half
    feats = chunks * width

    def cols(z):
        return pl.ds(pl.multiple_of(z * width, width), width)

    def w_cols(z, which):
        return pl.ds(pl.multiple_of(z * width + which * half, half), half)

    def fetch(z, carry):
        for i, pair in enumerate(acts):
            at = pl.ds(i * rows, rows)
            for k, (source, buf) in enumerate(zip(pair, (p_s, g_s))):
                pltpu.make_async_copy(
                    source.at[:, cols(z)], buf.at[at, cols(z)], in_sem.at[k, z]
                ).start()
        for source, which in ((w_own, core), (w_oth, 1 - core)):
            pltpu.make_async_copy(
                source.at[z, pl.ds(0, hidden), :], wi_s.at[:, w_cols(z, which)], in_sem.at[2, z]
            ).start()
            pltpu.make_async_copy(
                source.at[z, pl.ds(hidden, hidden), :],
                wo_s.at[:, w_cols(z, which)],
                in_sem.at[3, z],
            ).start()
        return carry

    lax.fori_loop(0, chunks, fetch, 0)
    h_s[...] = jnp.zeros_like(h_s)
    ga_s[...] = jnp.zeros_like(ga_s)
    sq_s[...] = jnp.zeros_like(sq_s)

    def first(z, carry):
        for k, buf in enumerate((p_s, g_s, wi_s, wo_s)):
            view = buf.at[:, cols(z)]
            pltpu.make_async_copy(view, view, in_sem.at[k, z]).wait()
        p = p_s[:, cols(z)]
        h_s[...] += nt(p, wi_s[:, cols(z)])
        ga_s[...] += nt(g_s[:, cols(z)], wo_s[:, cols(z)])
        pf = p.astype(jnp.float32)
        sq_s[...] += jnp.sum(pf * pf, axis=1, keepdims=True)
        return carry

    lax.fori_loop(0, chunks, first, 0)
    inv = lax.rsqrt(sq_s[...] * (1.0 / feats) + 1e-05)
    v = h_s[...] * inv
    v2 = v * v
    t = jnp.tanh(0.7978845608 * v * (1.0 + 0.044715 * v2))
    up = 0.5 * (1.0 + t)
    a = (v * up).astype(jnp.bfloat16)
    slope = up + 0.5 * v * (1.0 - t * t) * (0.7978845608 * (1.0 + 0.134145 * v2))
    b = (ga_s[...] * slope * inv).astype(jnp.bfloat16)
    act[...] = a
    gp[...] = b
    act_t[...] = a.T
    gp_t[...] = b.T

    def second(z, carry):
        wi = wi_s[:, cols(z)]
        d_s[:, cols(z)] = nn(act[...], wo_s[:, cols(z)]).astype(jnp.bfloat16)
        n_s[:, cols(z)] = nn(gp[...], wi).astype(jnp.bfloat16)
        go_s[:, cols(z)] = nn(act_t[...], g_s[:, cols(z)]).astype(jnp.bfloat16)
        gi = nn(gp_t[...], p_s[:, cols(z)])
        gi_s[:, cols(z)] = gi.astype(jnp.bfloat16)
        gain[:, cols(z)] = jnp.sum(gi * wi.astype(jnp.float32), axis=0, keepdims=True)
        for i, pair in enumerate(outs):
            at = pl.ds(i * rows, rows)
            for k, (dest, buf) in enumerate(zip(pair, (d_s, n_s))):
                pltpu.make_async_copy(
                    buf.at[at, cols(z)], dest.at[:, cols(z)], out_sem.at[k, z]
                ).start()
        for dest, which in ((g_own, core), (g_oth, 1 - core)):
            pltpu.make_async_copy(
                gi_s.at[:, w_cols(z, which)], dest.at[z, pl.ds(0, hidden), :], out_sem.at[2, z]
            ).start()
            pltpu.make_async_copy(
                go_s.at[:, w_cols(z, which)], dest.at[z, pl.ds(hidden, hidden), :], out_sem.at[3, z]
            ).start()
        return carry

    lax.fori_loop(0, chunks, second, 0)

    def drain(z, carry):
        for k, buf in enumerate((d_s, n_s, gi_s, go_s)):
            view = buf.at[:, cols(z)]
            pltpu.make_async_copy(view, view, out_sem.at[k, z]).wait()
        return carry

    lax.fori_loop(0, chunks, drain, 0)


def block(acts, w_own, w_oth):
    rows, feats = acts[0].shape
    chunks, hidden2, half = w_own.shape
    hidden = hidden2 // 2
    total = 4 * rows
    bf = jnp.bfloat16
    anywhere = pl.BlockSpec(memory_space=pl.ANY)
    flops = 12 * total * feats * hidden
    return pl.pallas_call(
        functools.partial(block_kernel, chunks),
        out_shape=[jax.ShapeDtypeStruct(act.shape, bf) for act in acts]
        + [jax.ShapeDtypeStruct(w_own.shape, bf)] * 2
        + [jax.ShapeDtypeStruct((1, feats), jnp.float32)],
        in_specs=[anywhere] * 10,
        out_specs=[anywhere] * 10 + [pl.BlockSpec(memory_space=pltpu.VMEM)],
        scratch_shapes=[pltpu.VMEM((total, feats), bf)] * 2
        + [pltpu.VMEM((hidden, feats), bf)] * 2
        + [pltpu.VMEM((total, feats), bf)] * 2
        + [pltpu.VMEM((hidden, feats), bf)] * 2
        + [pltpu.VMEM((total, hidden), jnp.float32)] * 2
        + [pltpu.VMEM((total, 1), jnp.float32)]
        + [pltpu.VMEM((total, hidden), bf)] * 2
        + [pltpu.VMEM((hidden, total), bf)] * 2
        + [pltpu.SemaphoreType.DMA((4, chunks)), pltpu.SemaphoreType.DMA((4, chunks))],
        compiler_params=pltpu.CompilerParams(vmem_limit_bytes=48 * 1024 * 1024),
        cost_estimate=pl.CostEstimate(
            flops=flops, bytes_accessed=8 * (total + hidden) * feats * 2, transcendentals=0
        ),
    )(*acts, w_own, w_oth)


def add_all(parts):
    total = parts[0].astype(jnp.float32)
    for part in parts[1:]:
        total = total + part.astype(jnp.float32)
    return total


def gather_plane(acts):
    parts = [acts] + [shift(acts, first=d) for d in (1, 2, 3)]
    p0 = jnp.concatenate([part[0] for part in parts], axis=0)
    g0 = jnp.concatenate([part[1] for part in parts], axis=0)
    p0, g0 = lax.optimization_barrier((p0, g0))
    p1, g3 = shift(p0, second=1), shift(g0, second=-1)
    g1, p3 = shift(g0, second=1), shift(p0, second=-1)
    p1, g3, g1, p3 = lax.optimization_barrier((p1, g3, g1, p3))
    p2, g2 = shift(p1, second=1), shift(g3, second=-1)
    return [p0, p1, p2, p3, g0, g1, g2, g3]


def swapped(value, moves):
    for move in moves:
        value = value + lax.ppermute(
            value, AXES, [(linear(*p), linear(*move(p))) for p in places()]
        )
    return value


def all_moves():
    moves = [lambda p, k=k: (p[0], p[1] ^ k, p[2], p[3]) for k in (1, 2)]
    moves += [lambda p, k=k: (p[0], p[1], p[2] ^ k, p[3]) for k in (1, 2)]
    moves += [lambda p, k=k: (p[0] ^ k, p[1], p[2], p[3]) for k in (1, 2, 4)]
    return moves + [lambda p: (p[0], p[1], p[2], 1 - p[3])]


def rounded_sum(*parts):
    return add_all(parts).astype(jnp.bfloat16)


def scatter_plane(outs, g_own, g_oth, gain):
    d0, d1, d2, d3, n0, n1, n2, n3 = outs
    tie = lax.optimization_barrier
    moves = all_moves()
    d2, n2 = shift(d2, second=-1), shift(n2, second=1)
    n1, d3 = shift(n1, second=-1), shift(d3, second=1)
    d2, n2, g_oth = tie((d2, n2, other_core(g_oth)))
    mine = rounded_sum(g_own, g_oth)
    weight_sum = lax.psum_scatter(mine, "z", scatter_dimension=0, tiled=False)
    d1, n3 = rounded_sum(d1, d2), rounded_sum(n3, n2)
    d1, n3, n1, d3, gain, _ = tie((d1, n3, n1, d3, gain, mine))
    d1, n3, gain = tie((shift(d1, second=-1), shift(n3, second=1), swapped(gain, moves[:2])))
    both = jnp.stack([rounded_sum(d0, d1, d3), rounded_sum(n0, n1, n3)])
    rows = both.shape[1] // 4
    both = [both[:, d * rows : (d + 1) * rows] for d in range(4)]
    arrived = [shift(both[d], first=-d) for d in (1, 2, 3)]
    *arrived, gain, weight_sum = tie((*arrived, swapped(gain, moves[2:4]), weight_sum))
    return add_all([both[0], *arrived]), swapped(gain, moves[4:]), weight_sum


def shards(stream, doc_start, norm_gain, weight_in, weight_out, upstream):
    tok_rows, feats = stream.shape
    groups = tok_rows // 4
    hidden = weight_out.shape[0]
    k_rows = weight_in.shape[0]
    bf = jnp.bfloat16
    seq = lax.axis_index("z") * 2 + lax.axis_index("yl")
    gain = lax.dynamic_slice(norm_gain, (seq * k_rows,), (k_rows,))

    scaled_in = (weight_in.T.astype(jnp.float32) * gain[None, :]).astype(bf)
    both = swap_low(jnp.concatenate([scaled_in, weight_out], axis=0))
    w_own = lax.all_gather(both, "z", axis=0, tiled=False)

    starts = doc_start.reshape(groups, 4).astype(jnp.float32)
    keep = jnp.cumprod(1.0 - starts, axis=1).reshape(tok_rows)
    group_of = lax.broadcasted_iota(jnp.int32, (groups, tok_rows), 1) // 4
    here = lax.broadcasted_iota(jnp.int32, (groups, tok_rows), 0)
    pool = jnp.where(group_of == here, 0.25, 0.0).astype(bf)
    pooled = nn(pool, stream).astype(bf)
    pick = jnp.where(group_of == here, keep[None, :], 0.0).astype(bf)
    group_sums = nn(pick, upstream).astype(bf)
    following = from_behind(group_sums[:1], -1)
    grad_coarse = jnp.concatenate([group_sums[1:], following], axis=0)

    acts = jnp.stack([pooled, grad_coarse], axis=0)
    blocks = gather_plane(acts)
    w_own = lax.optimization_barrier((w_own, blocks[1], blocks[3]))[0]
    w_oth = other_core(w_own)
    results = block(blocks, w_own, w_oth)
    outs, (g_own, g_oth, gain_part) = results[:8], results[8:]
    (down_sum, scaled), grad_gain, grads = scatter_plane(
        outs, g_own, g_oth, gain_part[0] / norm_gain
    )
    grads = swap_low(grads)
    grad_weight_in = (grads[:hidden].astype(jnp.float32) * gain[None, :]).T
    grad_weight_out = grads[hidden:].astype(jnp.float32)
    pooled_f = pooled.astype(jnp.float32)
    inv_sq = 1.0 / (jnp.mean(pooled_f * pooled_f, axis=1, keepdims=True) + 1e-05)
    coarse = (pooled_f + down_sum).astype(bf)
    carried = from_behind(coarse[groups - 1 :], 1)
    earlier = jnp.concatenate([carried, coarse[:-1]], axis=0)
    mixed_stream = (stream.astype(jnp.float32) + nn(pick.T, earlier)).astype(bf)
    grad_pooled = grad_coarse.astype(jnp.float32) + (
        scaled - pooled_f * inv_sq * jnp.mean(scaled * pooled_f, axis=1, keepdims=True)
    )
    grad_stream = (upstream.astype(jnp.float32) + nn(pool.T, grad_pooled.astype(bf))).astype(bf)
    return (mixed_stream, grad_stream, grad_gain, grad_weight_in, grad_weight_out)


def solution(mesh):
    fine = Mesh(mesh.devices.reshape(NZ, 2, NX, 2, 2), AXES)
    rows = P(AXES, None)
    seq, mp = ("z", "yl"), ("x", "yh", "c")
    in_specs = (rows, P(AXES), P(), P(seq, mp), P(mp, seq), rows)
    out_specs = (rows, rows, P(), P(seq, mp), P(mp, seq))
    return jax.shard_map(shards, mesh=fine, in_specs=in_specs, out_specs=out_specs, check_vma=False)
```

```python
import functools

import jax
import jax.numpy as jnp
from jax import lax
from jax.experimental import pallas as pl
from jax.experimental.pallas import tpu as pltpu
from jax.sharding import Mesh, PartitionSpec as P

AXES = ("z", "yl", "x", "yh", "c")
NZ, NY, NX = 8, 4, 4


def linear(z, y, x, c):
    return (((z * 2 + y % 2) * NX + x) * 2 + y // 2) * 2 + c


def places():
    return [
        (z, y, x, c) for z in range(NZ) for y in range(NY) for x in range(NX) for c in range(2)
    ]


def shift(value, first=0, second=0):
    pairs = []
    for z, y, x, c in places():
        dy, dx = (second, first) if c else (first, second)
        pairs.append((linear(z, y, x, c), linear(z, (y + dy) % NY, (x + dx) % NX, c)))
    return lax.ppermute(value, AXES, pairs)


def other_core(value):
    pairs = [(linear(z, y, x, c), linear(z, y, x, 1 - c)) for z, y, x, c in places()]
    return lax.ppermute(value, AXES, pairs)


def swap_low(value):
    pairs = [
        (linear(z, y, x, c), linear(z, (y // 2) * 2 + c, x, y % 2)) for z, y, x, c in places()
    ]
    return lax.ppermute(value, AXES, pairs)


def from_behind(value, by):
    count = NZ * NY * NX * 2
    pairs = [(i, i + by) for i in range(count) if 0 <= i + by < count]
    return lax.ppermute(value, AXES, pairs)


def nt(a, b):
    return lax.dot_general(a, b, (((1,), (1,)), ((), ())), preferred_element_type=jnp.float32)


def nn(a, b):
    return jnp.dot(a, b, preferred_element_type=jnp.float32)


def block_kernel(chunks, *refs):
    acts = list(zip(refs[:4], refs[4:8]))
    w_own, w_oth = refs[8:10]
    outs = list(zip(refs[10:14], refs[14:18]))
    g_own, g_oth, gain = refs[18:21]
    (p_s, g_s, wi_s, wo_s, d_s, n_s, gi_s, go_s, h_s, ga_s, sq_s, act, gp, act_t, gp_t, in_sem,
     out_sem) = refs[21:]
    core = lax.axis_index("c")
    rows = refs[0].shape[0]
    hidden = wi_s.shape[0]
    half = w_own.shape[2]
    width = 2 * half
    feats = chunks * width

    def cols(z):
        return pl.ds(pl.multiple_of(z * width, width), width)

    def w_cols(z, which):
        return pl.ds(pl.multiple_of(z * width + which * half, half), half)

    def fetch(z, carry):
        for i, pair in enumerate(acts):
            at = pl.ds(i * rows, rows)
            for k, (source, buf) in enumerate(zip(pair, (p_s, g_s))):
                pltpu.make_async_copy(
                    source.at[:, cols(z)], buf.at[at, cols(z)], in_sem.at[k, z]
                ).start()
        for source, which in ((w_own, core), (w_oth, 1 - core)):
            pltpu.make_async_copy(
                source.at[z, pl.ds(0, hidden), :], wi_s.at[:, w_cols(z, which)], in_sem.at[2, z]
            ).start()
            pltpu.make_async_copy(
                source.at[z, pl.ds(hidden, hidden), :],
                wo_s.at[:, w_cols(z, which)],
                in_sem.at[3, z],
            ).start()
        return carry

    lax.fori_loop(0, chunks, fetch, 0)
    h_s[...] = jnp.zeros_like(h_s)
    ga_s[...] = jnp.zeros_like(ga_s)
    sq_s[...] = jnp.zeros_like(sq_s)

    def first(z, carry):
        for k, buf in enumerate((p_s, g_s, wi_s, wo_s)):
            view = buf.at[:, cols(z)]
            pltpu.make_async_copy(view, view, in_sem.at[k, z]).wait()
        p = p_s[:, cols(z)]
        h_s[...] += nt(p, wi_s[:, cols(z)])
        ga_s[...] += nt(g_s[:, cols(z)], wo_s[:, cols(z)])
        pf = p.astype(jnp.float32)
        sq_s[...] += jnp.sum(pf * pf, axis=1, keepdims=True)
        return carry

    lax.fori_loop(0, chunks, first, 0)
    inv = lax.rsqrt(sq_s[...] * (1.0 / feats) + 1e-05)
    v = h_s[...] * inv
    v2 = v * v
    t = jnp.tanh(0.7978845608 * v * (1.0 + 0.044715 * v2))
    up = 0.5 * (1.0 + t)
    a = (v * up).astype(jnp.bfloat16)
    slope = up + 0.5 * v * (1.0 - t * t) * (0.7978845608 * (1.0 + 0.134145 * v2))
    b = (ga_s[...] * slope * inv).astype(jnp.bfloat16)
    act[...] = a
    gp[...] = b
    act_t[...] = a.T
    gp_t[...] = b.T

    def second(z, carry):
        wi = wi_s[:, cols(z)]
        d_s[:, cols(z)] = nn(act[...], wo_s[:, cols(z)]).astype(jnp.bfloat16)
        n_s[:, cols(z)] = nn(gp[...], wi).astype(jnp.bfloat16)
        go_s[:, cols(z)] = nn(act_t[...], g_s[:, cols(z)]).astype(jnp.bfloat16)
        gi = nn(gp_t[...], p_s[:, cols(z)])
        gi_s[:, cols(z)] = gi.astype(jnp.bfloat16)
        gain[:, cols(z)] = jnp.sum(gi * wi.astype(jnp.float32), axis=0, keepdims=True)
        for i, pair in enumerate(outs):
            at = pl.ds(i * rows, rows)
            for k, (dest, buf) in enumerate(zip(pair, (d_s, n_s))):
                pltpu.make_async_copy(
                    buf.at[at, cols(z)], dest.at[:, cols(z)], out_sem.at[k, z]
                ).start()
        for dest, which in ((g_own, core), (g_oth, 1 - core)):
            pltpu.make_async_copy(
                gi_s.at[:, w_cols(z, which)], dest.at[z, pl.ds(0, hidden), :], out_sem.at[2, z]
            ).start()
            pltpu.make_async_copy(
                go_s.at[:, w_cols(z, which)], dest.at[z, pl.ds(hidden, hidden), :], out_sem.at[3, z]
            ).start()
        return carry

    lax.fori_loop(0, chunks, second, 0)

    def drain(z, carry):
        for k, buf in enumerate((d_s, n_s, gi_s, go_s)):
            view = buf.at[:, cols(z)]
            pltpu.make_async_copy(view, view, out_sem.at[k, z]).wait()
        return carry

    lax.fori_loop(0, chunks, drain, 0)


def block(acts, w_own, w_oth):
    rows, feats = acts[0].shape
    chunks, hidden2, half = w_own.shape
    hidden = hidden2 // 2
    total = 4 * rows
    bf = jnp.bfloat16
    anywhere = pl.BlockSpec(memory_space=pl.ANY)
    flops = 12 * total * feats * hidden
    return pl.pallas_call(
        functools.partial(block_kernel, chunks),
        out_shape=[jax.ShapeDtypeStruct(act.shape, bf) for act in acts]
        + [jax.ShapeDtypeStruct(w_own.shape, bf)] * 2
        + [jax.ShapeDtypeStruct((1, feats), jnp.float32)],
        in_specs=[anywhere] * 10,
        out_specs=[anywhere] * 10 + [pl.BlockSpec(memory_space=pltpu.VMEM)],
        scratch_shapes=[pltpu.VMEM((total, feats), bf)] * 2
        + [pltpu.VMEM((hidden, feats), bf)] * 2
        + [pltpu.VMEM((total, feats), bf)] * 2
        + [pltpu.VMEM((hidden, feats), bf)] * 2
        + [pltpu.VMEM((total, hidden), jnp.float32)] * 2
        + [pltpu.VMEM((total, 1), jnp.float32)]
        + [pltpu.VMEM((total, hidden), bf)] * 2
        + [pltpu.VMEM((hidden, total), bf)] * 2
        + [pltpu.SemaphoreType.DMA((4, chunks)), pltpu.SemaphoreType.DMA((4, chunks))],
        compiler_params=pltpu.CompilerParams(vmem_limit_bytes=48 * 1024 * 1024),
        cost_estimate=pl.CostEstimate(
            flops=flops, bytes_accessed=8 * (total + hidden) * feats * 2, transcendentals=0
        ),
    )(*acts, w_own, w_oth)


def add_all(parts):
    total = parts[0].astype(jnp.float32)
    for part in parts[1:]:
        total = total + part.astype(jnp.float32)
    return total


def gather_plane(acts):
    parts = [acts] + [shift(acts, first=d) for d in (1, 2, 3)]
    p0 = jnp.concatenate([part[0] for part in parts], axis=0)
    g0 = jnp.concatenate([part[1] for part in parts], axis=0)
    p0, g0 = lax.optimization_barrier((p0, g0))
    p1, g3 = shift(p0, second=1), shift(g0, second=-1)
    g1, p3 = shift(g0, second=1), shift(p0, second=-1)
    p1, g3, g1, p3 = lax.optimization_barrier((p1, g3, g1, p3))
    p2, g2 = shift(p1, second=1), shift(g3, second=-1)
    return [p0, p1, p2, p3, g0, g1, g2, g3]


def scatter_plane(outs, gain_part, weight_part):
    d0, d1, d2, d3, n0, n1, n2, n3 = outs
    bf = jnp.bfloat16
    d2, n2 = shift(d2, second=-1), shift(n2, second=1)
    n1, d3 = shift(n1, second=-1), shift(d3, second=1)
    d1, n3 = add_all([d1, d2]).astype(bf), add_all([n3, n2]).astype(bf)
    d1, n3, weight_part = lax.optimization_barrier((d1, n3, weight_part))
    weight_sum = lax.psum_scatter(weight_part, "z", scatter_dimension=0, tiled=False)
    d1, n3 = shift(d1, second=-1), shift(n3, second=1)
    gain = pair(pair(pair(pair(pair(gain_part, z=1), z=2), c=1), y=1), y=2)
    d1, d3, n1, n3, gain = lax.optimization_barrier((d1, d3, n1, n3, gain))
    both = jnp.stack([add_all([d0, d1, d3]).astype(bf), add_all([n0, n1, n3]).astype(bf)])
    rows = both.shape[1] // 4
    both = [both[:, d * rows : (d + 1) * rows] for d in range(4)]
    arrived = [shift(both[d], first=-d) for d in (1, 2, 3)] + [weight_sum]
    gain = pair(pair(pair(gain, x=1), x=2), z=4)
    *arrived, weight_sum, gain = lax.optimization_barrier([*arrived, gain])
    return add_all([both[0], *arrived]), gain, weight_sum


def pair(value, z=0, y=0, x=0, c=0):
    pairs = [(linear(*p), linear(p[0] ^ z, p[1] ^ y, p[2] ^ x, p[3] ^ c)) for p in places()]
    return value + lax.ppermute(value, AXES, pairs)


def shards(stream, doc_start, norm_gain, weight_in, weight_out, upstream):
    tok_rows, feats = stream.shape
    groups = tok_rows // 4
    hidden = weight_out.shape[0]
    k_rows = weight_in.shape[0]
    bf = jnp.bfloat16
    seq = lax.axis_index("z") * 2 + lax.axis_index("yl")
    gain = lax.dynamic_slice(norm_gain, (seq * k_rows,), (k_rows,))

    scaled_in = (weight_in.T.astype(jnp.float32) * gain[None, :]).astype(bf)
    both = swap_low(jnp.concatenate([scaled_in, weight_out], axis=0))
    w_own = lax.all_gather(both, "z", axis=0, tiled=False)

    starts = doc_start.reshape(groups, 4).astype(jnp.float32)
    keep = jnp.cumprod(1.0 - starts, axis=1).reshape(tok_rows)
    group_of = lax.broadcasted_iota(jnp.int32, (groups, tok_rows), 1) // 4
    here = lax.broadcasted_iota(jnp.int32, (groups, tok_rows), 0)
    pool = jnp.where(group_of == here, 0.25, 0.0).astype(bf)
    pooled = nn(pool, stream).astype(bf)
    pick = jnp.where(group_of == here, keep[None, :], 0.0).astype(bf)
    group_sums = nn(pick, upstream).astype(bf)
    following = from_behind(group_sums[:1], -1)
    grad_coarse = jnp.concatenate([group_sums[1:], following], axis=0)

    acts = jnp.stack([pooled, grad_coarse], axis=0)
    blocks = gather_plane(acts)
    w_own = lax.optimization_barrier((w_own, blocks[1], blocks[3]))[0]
    w_oth = other_core(w_own)
    results = block(blocks, w_own, w_oth)
    outs, (g_own, g_oth, gain_part) = results[:8], results[8:]

    mine = (g_own.astype(jnp.float32) + other_core(g_oth).astype(jnp.float32)).astype(bf)
    (down_sum, scaled), grad_gain, grads = scatter_plane(outs, gain_part[0] / norm_gain, mine)
    grads = swap_low(grads)
    grad_weight_in = (grads[:hidden].astype(jnp.float32) * gain[None, :]).T
    grad_weight_out = grads[hidden:].astype(jnp.float32)
    pooled_f = pooled.astype(jnp.float32)
    inv_sq = 1.0 / (jnp.mean(pooled_f * pooled_f, axis=1, keepdims=True) + 1e-05)
    coarse = (pooled_f + down_sum).astype(bf)
    carried = from_behind(coarse[groups - 1 :], 1)
    earlier = jnp.concatenate([carried, coarse[:-1]], axis=0)
    mixed_stream = (stream.astype(jnp.float32) + nn(pick.T, earlier)).astype(bf)
    grad_pooled = grad_coarse.astype(jnp.float32) + (
        scaled - pooled_f * inv_sq * jnp.mean(scaled * pooled_f, axis=1, keepdims=True)
    )
    grad_stream = (upstream.astype(jnp.float32) + nn(pool.T, grad_pooled.astype(bf))).astype(bf)
    return (mixed_stream, grad_stream, grad_gain, grad_weight_in, grad_weight_out)


def solution(mesh):
    fine = Mesh(mesh.devices.reshape(NZ, 2, NX, 2, 2), AXES)
    rows = P(AXES, None)
    seq, mp = ("z", "yl"), ("x", "yh", "c")
    in_specs = (rows, P(AXES), P(), P(seq, mp), P(mp, seq), rows)
    out_specs = (rows, rows, P(), P(seq, mp), P(mp, seq))
    return jax.shard_map(shards, mesh=fine, in_specs=in_specs, out_specs=out_specs, check_vma=False)
```

```python
import functools

import jax
import jax.numpy as jnp
from jax import lax
from jax.experimental import pallas as pl
from jax.experimental.pallas import tpu as pltpu
from jax.sharding import Mesh, PartitionSpec as P

AXES = ("z", "yl", "x", "yh", "c")
NZ, NY, NX = 8, 4, 4


def linear(z, y, x, c):
    return (((z * 2 + y % 2) * NX + x) * 2 + y // 2) * 2 + c


def places():
    return [
        (z, y, x, c) for z in range(NZ) for y in range(NY) for x in range(NX) for c in range(2)
    ]


def shift(value, first=0, second=0):
    pairs = []
    for z, y, x, c in places():
        dy, dx = (second, first) if c else (first, second)
        pairs.append((linear(z, y, x, c), linear(z, (y + dy) % NY, (x + dx) % NX, c)))
    return lax.ppermute(value, AXES, pairs)


def other_core(value):
    pairs = [(linear(z, y, x, c), linear(z, y, x, 1 - c)) for z, y, x, c in places()]
    return lax.ppermute(value, AXES, pairs)


def swap_low(value):
    pairs = [
        (linear(z, y, x, c), linear(z, (y // 2) * 2 + c, x, y % 2)) for z, y, x, c in places()
    ]
    return lax.ppermute(value, AXES, pairs)


def from_behind(value, by):
    count = NZ * NY * NX * 2
    pairs = [(i, i + by) for i in range(count) if 0 <= i + by < count]
    return lax.ppermute(value, AXES, pairs)


def nt(a, b):
    return lax.dot_general(a, b, (((1,), (1,)), ((), ())), preferred_element_type=jnp.float32)


def nn(a, b):
    return jnp.dot(a, b, preferred_element_type=jnp.float32)


def block_kernel(chunks, *refs):
    acts = list(zip(refs[:4], refs[4:8]))
    w_own, w_oth = refs[8:10]
    outs = list(zip(refs[10:14], refs[14:18]))
    g_own, g_oth, gain = refs[18:21]
    (p_s, g_s, wi_s, wo_s, d_s, n_s, gi_s, go_s, h_s, ga_s, sq_s, act, gp, act_t, gp_t, in_sem,
     out_sem) = refs[21:]
    core = lax.axis_index("c")
    rows = refs[0].shape[0]
    hidden = wi_s.shape[0]
    half = w_own.shape[2]
    width = 2 * half
    feats = chunks * width

    def cols(z):
        return pl.ds(pl.multiple_of(z * width, width), width)

    def w_cols(z, which):
        return pl.ds(pl.multiple_of(z * width + which * half, half), half)

    def fetch(z, carry):
        for i, pair in enumerate(acts):
            at = pl.ds(i * rows, rows)
            for k, (source, buf) in enumerate(zip(pair, (p_s, g_s))):
                pltpu.make_async_copy(
                    source.at[:, cols(z)], buf.at[at, cols(z)], in_sem.at[k, z]
                ).start()
        for source, which in ((w_own, core), (w_oth, 1 - core)):
            pltpu.make_async_copy(
                source.at[z, pl.ds(0, hidden), :], wi_s.at[:, w_cols(z, which)], in_sem.at[2, z]
            ).start()
            pltpu.make_async_copy(
                source.at[z, pl.ds(hidden, hidden), :],
                wo_s.at[:, w_cols(z, which)],
                in_sem.at[3, z],
            ).start()
        return carry

    lax.fori_loop(0, chunks, fetch, 0)
    h_s[...] = jnp.zeros_like(h_s)
    ga_s[...] = jnp.zeros_like(ga_s)
    sq_s[...] = jnp.zeros_like(sq_s)

    def first(z, carry):
        for k, buf in enumerate((p_s, g_s, wi_s, wo_s)):
            view = buf.at[:, cols(z)]
            pltpu.make_async_copy(view, view, in_sem.at[k, z]).wait()
        p = p_s[:, cols(z)]
        h_s[...] += nt(p, wi_s[:, cols(z)])
        ga_s[...] += nt(g_s[:, cols(z)], wo_s[:, cols(z)])
        pf = p.astype(jnp.float32)
        sq_s[...] += jnp.sum(pf * pf, axis=1, keepdims=True)
        return carry

    lax.fori_loop(0, chunks, first, 0)
    inv = lax.rsqrt(sq_s[...] * (1.0 / feats) + 1e-05)
    v = h_s[...] * inv
    v2 = v * v
    t = jnp.tanh(0.7978845608 * v * (1.0 + 0.044715 * v2))
    up = 0.5 * (1.0 + t)
    a = (v * up).astype(jnp.bfloat16)
    slope = up + 0.5 * v * (1.0 - t * t) * (0.7978845608 * (1.0 + 0.134145 * v2))
    b = (ga_s[...] * slope * inv).astype(jnp.bfloat16)
    act[...] = a
    gp[...] = b
    act_t[...] = a.T
    gp_t[...] = b.T

    def second(z, carry):
        wi = wi_s[:, cols(z)]
        d_s[:, cols(z)] = nn(act[...], wo_s[:, cols(z)]).astype(jnp.bfloat16)
        n_s[:, cols(z)] = nn(gp[...], wi).astype(jnp.bfloat16)
        go_s[:, cols(z)] = nn(act_t[...], g_s[:, cols(z)]).astype(jnp.bfloat16)
        gi = nn(gp_t[...], p_s[:, cols(z)])
        gi_s[:, cols(z)] = gi.astype(jnp.bfloat16)
        gain[:, cols(z)] = jnp.sum(gi * wi.astype(jnp.float32), axis=0, keepdims=True)
        for i, pair in enumerate(outs):
            at = pl.ds(i * rows, rows)
            for k, (dest, buf) in enumerate(zip(pair, (d_s, n_s))):
                pltpu.make_async_copy(
                    buf.at[at, cols(z)], dest.at[:, cols(z)], out_sem.at[k, z]
                ).start()
        for dest, which in ((g_own, core), (g_oth, 1 - core)):
            pltpu.make_async_copy(
                gi_s.at[:, w_cols(z, which)], dest.at[z, pl.ds(0, hidden), :], out_sem.at[2, z]
            ).start()
            pltpu.make_async_copy(
                go_s.at[:, w_cols(z, which)], dest.at[z, pl.ds(hidden, hidden), :], out_sem.at[3, z]
            ).start()
        return carry

    lax.fori_loop(0, chunks, second, 0)

    def drain(z, carry):
        for k, buf in enumerate((d_s, n_s, gi_s, go_s)):
            view = buf.at[:, cols(z)]
            pltpu.make_async_copy(view, view, out_sem.at[k, z]).wait()
        return carry

    lax.fori_loop(0, chunks, drain, 0)


def block(acts, w_own, w_oth):
    rows, feats = acts[0].shape
    chunks, hidden2, half = w_own.shape
    hidden = hidden2 // 2
    total = 4 * rows
    bf = jnp.bfloat16
    anywhere = pl.BlockSpec(memory_space=pl.ANY)
    flops = 12 * total * feats * hidden
    return pl.pallas_call(
        functools.partial(block_kernel, chunks),
        out_shape=[jax.ShapeDtypeStruct(act.shape, bf) for act in acts]
        + [jax.ShapeDtypeStruct(w_own.shape, bf)] * 2
        + [jax.ShapeDtypeStruct((1, feats), jnp.float32)],
        in_specs=[anywhere] * 10,
        out_specs=[anywhere] * 10 + [pl.BlockSpec(memory_space=pltpu.VMEM)],
        scratch_shapes=[pltpu.VMEM((total, feats), bf)] * 2
        + [pltpu.VMEM((hidden, feats), bf)] * 2
        + [pltpu.VMEM((total, feats), bf)] * 2
        + [pltpu.VMEM((hidden, feats), bf)] * 2
        + [pltpu.VMEM((total, hidden), jnp.float32)] * 2
        + [pltpu.VMEM((total, 1), jnp.float32)]
        + [pltpu.VMEM((total, hidden), bf)] * 2
        + [pltpu.VMEM((hidden, total), bf)] * 2
        + [pltpu.SemaphoreType.DMA((4, chunks)), pltpu.SemaphoreType.DMA((4, chunks))],
        compiler_params=pltpu.CompilerParams(vmem_limit_bytes=48 * 1024 * 1024),
        cost_estimate=pl.CostEstimate(
            flops=flops, bytes_accessed=8 * (total + hidden) * feats * 2, transcendentals=0
        ),
    )(*acts, w_own, w_oth)


def add_all(parts):
    total = parts[0].astype(jnp.float32)
    for part in parts[1:]:
        total = total + part.astype(jnp.float32)
    return total


def gather_plane(acts):
    parts = [acts] + [shift(acts, first=d) for d in (1, 2, 3)]
    p0 = jnp.concatenate([part[0] for part in parts], axis=0)
    g0 = jnp.concatenate([part[1] for part in parts], axis=0)
    p0, g0 = lax.optimization_barrier((p0, g0))
    p1, g3 = shift(p0, second=1), shift(g0, second=-1)
    g1, p3 = shift(g0, second=1), shift(p0, second=-1)
    p1, g3, g1, p3 = lax.optimization_barrier((p1, g3, g1, p3))
    p2, g2 = shift(p1, second=1), shift(g3, second=-1)
    return [p0, p1, p2, p3, g0, g1, g2, g3]


def scatter_plane(outs, gain_part, weight_part):
    d0, d1, d2, d3, n0, n1, n2, n3 = outs
    bf = jnp.bfloat16
    d2, n2 = shift(d2, second=-1), shift(n2, second=1)
    n1, d3 = shift(n1, second=-1), shift(d3, second=1)
    d1, n3 = add_all([d1, d2]).astype(bf), add_all([n3, n2]).astype(bf)
    gain = pair(pair(pair(gain_part, z=1), z=2), z=4)
    d1, n3, weight_part, gain = lax.optimization_barrier((d1, n3, weight_part, gain))
    weight_sum = lax.psum_scatter(weight_part, "z", scatter_dimension=0, tiled=False)
    d1, n3 = shift(d1, second=-1), shift(n3, second=1)
    gain = pair(pair(pair(pair(pair(gain, c=1), y=1), y=2), x=1), x=2)
    d1, d3, n1, n3, gain = lax.optimization_barrier((d1, d3, n1, n3, gain))
    both = jnp.stack([add_all([d0, d1, d3]).astype(bf), add_all([n0, n1, n3]).astype(bf)])
    rows = both.shape[1] // 4
    both = [both[:, d * rows : (d + 1) * rows] for d in range(4)]
    arrived = [shift(both[d], first=-d) for d in (1, 2, 3)] + [weight_sum]
    *arrived, weight_sum = lax.optimization_barrier(arrived)
    return add_all([both[0], *arrived]), gain, weight_sum


def pair(value, z=0, y=0, x=0, c=0):
    pairs = [(linear(*p), linear(p[0] ^ z, p[1] ^ y, p[2] ^ x, p[3] ^ c)) for p in places()]
    return value + lax.ppermute(value, AXES, pairs)


def shards(stream, doc_start, norm_gain, weight_in, weight_out, upstream):
    tok_rows, feats = stream.shape
    groups = tok_rows // 4
    hidden = weight_out.shape[0]
    k_rows = weight_in.shape[0]
    bf = jnp.bfloat16
    seq = lax.axis_index("z") * 2 + lax.axis_index("yl")
    gain = lax.dynamic_slice(norm_gain, (seq * k_rows,), (k_rows,))

    scaled_in = (weight_in.T.astype(jnp.float32) * gain[None, :]).astype(bf)
    both = swap_low(jnp.concatenate([scaled_in, weight_out], axis=0))
    w_own = lax.all_gather(both, "z", axis=0, tiled=False)

    starts = doc_start.reshape(groups, 4).astype(jnp.float32)
    keep = jnp.cumprod(1.0 - starts, axis=1).reshape(tok_rows)
    group_of = lax.broadcasted_iota(jnp.int32, (groups, tok_rows), 1) // 4
    here = lax.broadcasted_iota(jnp.int32, (groups, tok_rows), 0)
    pool = jnp.where(group_of == here, 0.25, 0.0).astype(bf)
    pooled = nn(pool, stream).astype(bf)
    pick = jnp.where(group_of == here, keep[None, :], 0.0).astype(bf)
    group_sums = nn(pick, upstream).astype(bf)
    following = from_behind(group_sums[:1], -1)
    grad_coarse = jnp.concatenate([group_sums[1:], following], axis=0)

    acts = jnp.stack([pooled, grad_coarse], axis=0)
    blocks = gather_plane(acts)
    w_own = lax.optimization_barrier((w_own, blocks[1], blocks[3]))[0]
    w_oth = other_core(w_own)
    results = block(blocks, w_own, w_oth)
    outs, (g_own, g_oth, gain_part) = results[:8], results[8:]

    mine = (g_own.astype(jnp.float32) + other_core(g_oth).astype(jnp.float32)).astype(bf)
    (down_sum, scaled), grad_gain, grads = scatter_plane(outs, gain_part[0] / norm_gain, mine)
    grads = swap_low(grads)
    grad_weight_in = (grads[:hidden].astype(jnp.float32) * gain[None, :]).T
    grad_weight_out = grads[hidden:].astype(jnp.float32)
    pooled_f = pooled.astype(jnp.float32)
    inv_sq = 1.0 / (jnp.mean(pooled_f * pooled_f, axis=1, keepdims=True) + 1e-05)
    coarse = (pooled_f + down_sum).astype(bf)
    carried = from_behind(coarse[groups - 1 :], 1)
    earlier = jnp.concatenate([carried, coarse[:-1]], axis=0)
    mixed_stream = (stream.astype(jnp.float32) + nn(pick.T, earlier)).astype(bf)
    grad_pooled = grad_coarse.astype(jnp.float32) + (
        scaled - pooled_f * inv_sq * jnp.mean(scaled * pooled_f, axis=1, keepdims=True)
    )
    grad_stream = (upstream.astype(jnp.float32) + nn(pool.T, grad_pooled.astype(bf))).astype(bf)
    return (mixed_stream, grad_stream, grad_gain, grad_weight_in, grad_weight_out)


def solution(mesh):
    fine = Mesh(mesh.devices.reshape(NZ, 2, NX, 2, 2), AXES)
    rows = P(AXES, None)
    seq, mp = ("z", "yl"), ("x", "yh", "c")
    in_specs = (rows, P(AXES), P(), P(seq, mp), P(mp, seq), rows)
    out_specs = (rows, rows, P(), P(seq, mp), P(mp, seq))
    return jax.shard_map(shards, mesh=fine, in_specs=in_specs, out_specs=out_specs, check_vma=False)
```

```python
import functools

import jax
import jax.numpy as jnp
from jax import lax
from jax.experimental import pallas as pl
from jax.experimental.pallas import tpu as pltpu
from jax.sharding import Mesh, PartitionSpec as P

AXES = ("z", "yl", "x", "yh", "c")
NZ, NY, NX = 8, 4, 4


def linear(z, y, x, c):
    return (((z * 2 + y % 2) * NX + x) * 2 + y // 2) * 2 + c


def places():
    return [
        (z, y, x, c) for z in range(NZ) for y in range(NY) for x in range(NX) for c in range(2)
    ]


def shift(value, first=0, second=0):
    pairs = []
    for z, y, x, c in places():
        dy, dx = (second, first) if c else (first, second)
        pairs.append((linear(z, y, x, c), linear(z, (y + dy) % NY, (x + dx) % NX, c)))
    return lax.ppermute(value, AXES, pairs)


def other_core(value):
    pairs = [(linear(z, y, x, c), linear(z, y, x, 1 - c)) for z, y, x, c in places()]
    return lax.ppermute(value, AXES, pairs)


def swap_low(value):
    pairs = [
        (linear(z, y, x, c), linear(z, (y // 2) * 2 + c, x, y % 2)) for z, y, x, c in places()
    ]
    return lax.ppermute(value, AXES, pairs)


def from_behind(value, by):
    count = NZ * NY * NX * 2
    pairs = [(i, i + by) for i in range(count) if 0 <= i + by < count]
    return lax.ppermute(value, AXES, pairs)


def nt(a, b):
    return lax.dot_general(a, b, (((1,), (1,)), ((), ())), preferred_element_type=jnp.float32)


def nn(a, b):
    return jnp.dot(a, b, preferred_element_type=jnp.float32)


def block_kernel(chunks, *refs):
    acts = list(zip(refs[:4], refs[4:8]))
    w_own, w_oth = refs[8:10]
    outs = list(zip(refs[10:14], refs[14:18]))
    g_own, g_oth, gain = refs[18:21]
    (p_s, g_s, wi_s, wo_s, d_s, n_s, gi_s, go_s, h_s, ga_s, sq_s, act, gp, act_t, gp_t, in_sem,
     out_sem) = refs[21:]
    core = lax.axis_index("c")
    rows = refs[0].shape[0]
    hidden = wi_s.shape[0]
    half = w_own.shape[2]
    width = 2 * half
    feats = chunks * width

    def cols(z):
        return pl.ds(pl.multiple_of(z * width, width), width)

    def w_cols(z, which):
        return pl.ds(pl.multiple_of(z * width + which * half, half), half)

    def fetch(z, carry):
        for i, pair in enumerate(acts):
            at = pl.ds(i * rows, rows)
            for k, (source, buf) in enumerate(zip(pair, (p_s, g_s))):
                pltpu.make_async_copy(
                    source.at[:, cols(z)], buf.at[at, cols(z)], in_sem.at[k, z]
                ).start()
        for source, which in ((w_own, core), (w_oth, 1 - core)):
            pltpu.make_async_copy(
                source.at[z, pl.ds(0, hidden), :], wi_s.at[:, w_cols(z, which)], in_sem.at[2, z]
            ).start()
            pltpu.make_async_copy(
                source.at[z, pl.ds(hidden, hidden), :],
                wo_s.at[:, w_cols(z, which)],
                in_sem.at[3, z],
            ).start()
        return carry

    lax.fori_loop(0, chunks, fetch, 0)
    h_s[...] = jnp.zeros_like(h_s)
    ga_s[...] = jnp.zeros_like(ga_s)
    sq_s[...] = jnp.zeros_like(sq_s)

    def first(z, carry):
        for k, buf in enumerate((p_s, g_s, wi_s, wo_s)):
            view = buf.at[:, cols(z)]
            pltpu.make_async_copy(view, view, in_sem.at[k, z]).wait()
        p = p_s[:, cols(z)]
        h_s[...] += nt(p, wi_s[:, cols(z)])
        ga_s[...] += nt(g_s[:, cols(z)], wo_s[:, cols(z)])
        pf = p.astype(jnp.float32)
        sq_s[...] += jnp.sum(pf * pf, axis=1, keepdims=True)
        return carry

    lax.fori_loop(0, chunks, first, 0)
    inv = lax.rsqrt(sq_s[...] * (1.0 / feats) + 1e-05)
    v = h_s[...] * inv
    v2 = v * v
    t = jnp.tanh(0.7978845608 * v * (1.0 + 0.044715 * v2))
    up = 0.5 * (1.0 + t)
    a = (v * up).astype(jnp.bfloat16)
    slope = up + 0.5 * v * (1.0 - t * t) * (0.7978845608 * (1.0 + 0.134145 * v2))
    b = (ga_s[...] * slope * inv).astype(jnp.bfloat16)
    act[...] = a
    gp[...] = b
    act_t[...] = a.T
    gp_t[...] = b.T

    def second(z, carry):
        wi = wi_s[:, cols(z)]
        d_s[:, cols(z)] = nn(act[...], wo_s[:, cols(z)]).astype(jnp.bfloat16)
        n_s[:, cols(z)] = nn(gp[...], wi).astype(jnp.bfloat16)
        go_s[:, cols(z)] = nn(act_t[...], g_s[:, cols(z)]).astype(jnp.bfloat16)
        gi = nn(gp_t[...], p_s[:, cols(z)])
        gi_s[:, cols(z)] = gi.astype(jnp.bfloat16)
        gain[:, cols(z)] = jnp.sum(gi * wi.astype(jnp.float32), axis=0, keepdims=True)
        for i, pair in enumerate(outs):
            at = pl.ds(i * rows, rows)
            for k, (dest, buf) in enumerate(zip(pair, (d_s, n_s))):
                pltpu.make_async_copy(
                    buf.at[at, cols(z)], dest.at[:, cols(z)], out_sem.at[k, z]
                ).start()
        for dest, which in ((g_own, core), (g_oth, 1 - core)):
            pltpu.make_async_copy(
                gi_s.at[:, w_cols(z, which)], dest.at[z, pl.ds(0, hidden), :], out_sem.at[2, z]
            ).start()
            pltpu.make_async_copy(
                go_s.at[:, w_cols(z, which)], dest.at[z, pl.ds(hidden, hidden), :], out_sem.at[3, z]
            ).start()
        return carry

    lax.fori_loop(0, chunks, second, 0)

    def drain(z, carry):
        for k, buf in enumerate((d_s, n_s, gi_s, go_s)):
            view = buf.at[:, cols(z)]
            pltpu.make_async_copy(view, view, out_sem.at[k, z]).wait()
        return carry

    lax.fori_loop(0, chunks, drain, 0)


def block(acts, w_own, w_oth):
    rows, feats = acts[0].shape
    chunks, hidden2, half = w_own.shape
    hidden = hidden2 // 2
    total = 4 * rows
    bf = jnp.bfloat16
    anywhere = pl.BlockSpec(memory_space=pl.ANY)
    flops = 12 * total * feats * hidden
    return pl.pallas_call(
        functools.partial(block_kernel, chunks),
        out_shape=[jax.ShapeDtypeStruct(act.shape, bf) for act in acts]
        + [jax.ShapeDtypeStruct(w_own.shape, bf)] * 2
        + [jax.ShapeDtypeStruct((1, feats), jnp.float32)],
        in_specs=[anywhere] * 10,
        out_specs=[anywhere] * 10 + [pl.BlockSpec(memory_space=pltpu.VMEM)],
        scratch_shapes=[pltpu.VMEM((total, feats), bf)] * 2
        + [pltpu.VMEM((hidden, feats), bf)] * 2
        + [pltpu.VMEM((total, feats), bf)] * 2
        + [pltpu.VMEM((hidden, feats), bf)] * 2
        + [pltpu.VMEM((total, hidden), jnp.float32)] * 2
        + [pltpu.VMEM((total, 1), jnp.float32)]
        + [pltpu.VMEM((total, hidden), bf)] * 2
        + [pltpu.VMEM((hidden, total), bf)] * 2
        + [pltpu.SemaphoreType.DMA((4, chunks)), pltpu.SemaphoreType.DMA((4, chunks))],
        compiler_params=pltpu.CompilerParams(vmem_limit_bytes=48 * 1024 * 1024),
        cost_estimate=pl.CostEstimate(
            flops=flops, bytes_accessed=8 * (total + hidden) * feats * 2, transcendentals=0
        ),
    )(*acts, w_own, w_oth)


def add_all(parts):
    total = parts[0].astype(jnp.float32)
    for part in parts[1:]:
        total = total + part.astype(jnp.float32)
    return total


def gather_plane(acts):
    parts = [acts] + [shift(acts, first=d) for d in (1, 2, 3)]
    p0 = jnp.concatenate([part[0] for part in parts], axis=0)
    g0 = jnp.concatenate([part[1] for part in parts], axis=0)
    p0, g0 = lax.optimization_barrier((p0, g0))
    p1, g3 = shift(p0, second=1), shift(g0, second=-1)
    g1, p3 = shift(g0, second=1), shift(p0, second=-1)
    p1, g3, g1, p3 = lax.optimization_barrier((p1, g3, g1, p3))
    p2, g2 = shift(p1, second=1), shift(g3, second=-1)
    return [p0, p1, p2, p3, g0, g1, g2, g3]


def scatter_plane(outs, gain_part, weight_part):
    d0, d1, d2, d3, n0, n1, n2, n3 = outs
    bf = jnp.bfloat16
    d2, n2 = shift(d2, second=-1), shift(n2, second=1)
    n1, d3 = shift(n1, second=-1), shift(d3, second=1)
    d1, n3 = add_all([d1, d2]).astype(bf), add_all([n3, n2]).astype(bf)
    gain = pair(pair(pair(gain_part, z=1), z=2), z=4)
    d1, n3, weight_part, gain = lax.optimization_barrier((d1, n3, weight_part, gain))
    weight_sum = lax.psum_scatter(weight_part, "z", scatter_dimension=0, tiled=False)
    d1, n3 = shift(d1, second=-1), shift(n3, second=1)
    gain = pair(pair(gain, first=1), first=2)
    d1, d3, n1, n3, gain = lax.optimization_barrier((d1, d3, n1, n3, gain))
    both = jnp.stack([add_all([d0, d1, d3]).astype(bf), add_all([n0, n1, n3]).astype(bf)])
    rows = both.shape[1] // 4
    both = [both[:, d * rows : (d + 1) * rows] for d in range(4)]
    arrived = [shift(both[d], first=-d) for d in (1, 2, 3)] + [weight_sum]
    gain = pair(pair(pair(gain, second=1), second=2), c=1)
    *arrived, weight_sum, gain = lax.optimization_barrier([*arrived, gain])
    return add_all([both[0], *arrived]), gain, weight_sum


def pair(value, z=0, first=0, second=0, c=0):
    pairs = []
    for p in places():
        y, x = (second, first) if p[3] else (first, second)
        pairs.append((linear(*p), linear(p[0] ^ z, p[1] ^ y, p[2] ^ x, p[3] ^ c)))
    return value + lax.ppermute(value, AXES, pairs)


def shards(stream, doc_start, norm_gain, weight_in, weight_out, upstream):
    tok_rows, feats = stream.shape
    groups = tok_rows // 4
    hidden = weight_out.shape[0]
    k_rows = weight_in.shape[0]
    bf = jnp.bfloat16
    seq = lax.axis_index("z") * 2 + lax.axis_index("yl")
    gain = lax.dynamic_slice(norm_gain, (seq * k_rows,), (k_rows,))

    scaled_in = (weight_in.T.astype(jnp.float32) * gain[None, :]).astype(bf)
    both = swap_low(jnp.concatenate([scaled_in, weight_out], axis=0))
    w_own = lax.all_gather(both, "z", axis=0, tiled=False)

    starts = doc_start.reshape(groups, 4).astype(jnp.float32)
    keep = jnp.cumprod(1.0 - starts, axis=1).reshape(tok_rows)
    group_of = lax.broadcasted_iota(jnp.int32, (groups, tok_rows), 1) // 4
    here = lax.broadcasted_iota(jnp.int32, (groups, tok_rows), 0)
    pool = jnp.where(group_of == here, 0.25, 0.0).astype(bf)
    pooled = nn(pool, stream).astype(bf)
    pick = jnp.where(group_of == here, keep[None, :], 0.0).astype(bf)
    group_sums = nn(pick, upstream).astype(bf)
    following = from_behind(group_sums[:1], -1)
    grad_coarse = jnp.concatenate([group_sums[1:], following], axis=0)

    acts = jnp.stack([pooled, grad_coarse], axis=0)
    blocks = gather_plane(acts)
    w_own = lax.optimization_barrier((w_own, blocks[1], blocks[3]))[0]
    w_oth = other_core(w_own)
    results = block(blocks, w_own, w_oth)
    outs, (g_own, g_oth, gain_part) = results[:8], results[8:]

    mine = (g_own.astype(jnp.float32) + other_core(g_oth).astype(jnp.float32)).astype(bf)
    (down_sum, scaled), grad_gain, grads = scatter_plane(outs, gain_part[0] / norm_gain, mine)
    grads = swap_low(grads)
    grad_weight_in = (grads[:hidden].astype(jnp.float32) * gain[None, :]).T
    grad_weight_out = grads[hidden:].astype(jnp.float32)
    pooled_f = pooled.astype(jnp.float32)
    inv_sq = 1.0 / (jnp.mean(pooled_f * pooled_f, axis=1, keepdims=True) + 1e-05)
    coarse = (pooled_f + down_sum).astype(bf)
    carried = from_behind(coarse[groups - 1 :], 1)
    earlier = jnp.concatenate([carried, coarse[:-1]], axis=0)
    mixed_stream = (stream.astype(jnp.float32) + nn(pick.T, earlier)).astype(bf)
    grad_pooled = grad_coarse.astype(jnp.float32) + (
        scaled - pooled_f * inv_sq * jnp.mean(scaled * pooled_f, axis=1, keepdims=True)
    )
    grad_stream = (upstream.astype(jnp.float32) + nn(pool.T, grad_pooled.astype(bf))).astype(bf)
    return (mixed_stream, grad_stream, grad_gain, grad_weight_in, grad_weight_out)


def solution(mesh):
    fine = Mesh(mesh.devices.reshape(NZ, 2, NX, 2, 2), AXES)
    rows = P(AXES, None)
    seq, mp = ("z", "yl"), ("x", "yh", "c")
    in_specs = (rows, P(AXES), P(), P(seq, mp), P(mp, seq), rows)
    out_specs = (rows, rows, P(), P(seq, mp), P(mp, seq))
    return jax.shard_map(shards, mesh=fine, in_specs=in_specs, out_specs=out_specs, check_vma=False)
```

```python
import functools

import jax
import jax.numpy as jnp
from jax import lax
from jax.experimental import pallas as pl
from jax.experimental.pallas import tpu as pltpu
from jax.sharding import Mesh, PartitionSpec as P

AXES = ("z", "yl", "x", "yh", "c")
NZ, NY, NX = 8, 4, 4


def linear(z, y, x, c):
    return (((z * 2 + y % 2) * NX + x) * 2 + y // 2) * 2 + c


def places():
    return [
        (z, y, x, c) for z in range(NZ) for y in range(NY) for x in range(NX) for c in range(2)
    ]


def shift(value, first=0, second=0):
    pairs = []
    for z, y, x, c in places():
        dy, dx = (second, first) if c else (first, second)
        pairs.append((linear(z, y, x, c), linear(z, (y + dy) % NY, (x + dx) % NX, c)))
    return lax.ppermute(value, AXES, pairs)


def other_core(value):
    pairs = [(linear(z, y, x, c), linear(z, y, x, 1 - c)) for z, y, x, c in places()]
    return lax.ppermute(value, AXES, pairs)


def swap_low(value):
    pairs = [
        (linear(z, y, x, c), linear(z, (y // 2) * 2 + c, x, y % 2)) for z, y, x, c in places()
    ]
    return lax.ppermute(value, AXES, pairs)


def from_behind(value, by):
    count = NZ * NY * NX * 2
    pairs = [(i, i + by) for i in range(count) if 0 <= i + by < count]
    return lax.ppermute(value, AXES, pairs)


def nt(a, b):
    return lax.dot_general(a, b, (((1,), (1,)), ((), ())), preferred_element_type=jnp.float32)


def nn(a, b):
    return jnp.dot(a, b, preferred_element_type=jnp.float32)


def block_kernel(chunks, *refs):
    acts = list(zip(refs[:4], refs[4:8]))
    w_own, w_oth = refs[8:10]
    outs = list(zip(refs[10:14], refs[14:18]))
    g_own, g_oth, gain = refs[18:21]
    (p_s, g_s, wi_s, wo_s, d_s, n_s, gi_s, go_s, h_s, ga_s, sq_s, act, gp, act_t, gp_t, in_sem,
     out_sem) = refs[21:]
    core = lax.axis_index("c")
    rows = refs[0].shape[0]
    hidden = wi_s.shape[0]
    half = w_own.shape[2]
    width = 2 * half
    feats = chunks * width

    def cols(z):
        return pl.ds(pl.multiple_of(z * width, width), width)

    def w_cols(z, which):
        return pl.ds(pl.multiple_of(z * width + which * half, half), half)

    def fetch(z, carry):
        for i, pair in enumerate(acts):
            at = pl.ds(i * rows, rows)
            for k, (source, buf) in enumerate(zip(pair, (p_s, g_s))):
                pltpu.make_async_copy(
                    source.at[:, cols(z)], buf.at[at, cols(z)], in_sem.at[k, z]
                ).start()
        for source, which in ((w_own, core), (w_oth, 1 - core)):
            pltpu.make_async_copy(
                source.at[z, pl.ds(0, hidden), :], wi_s.at[:, w_cols(z, which)], in_sem.at[2, z]
            ).start()
            pltpu.make_async_copy(
                source.at[z, pl.ds(hidden, hidden), :],
                wo_s.at[:, w_cols(z, which)],
                in_sem.at[3, z],
            ).start()
        return carry

    lax.fori_loop(0, chunks, fetch, 0)
    h_s[...] = jnp.zeros_like(h_s)
    ga_s[...] = jnp.zeros_like(ga_s)
    sq_s[...] = jnp.zeros_like(sq_s)

    def first(z, carry):
        for k, buf in enumerate((p_s, g_s, wi_s, wo_s)):
            view = buf.at[:, cols(z)]
            pltpu.make_async_copy(view, view, in_sem.at[k, z]).wait()
        p = p_s[:, cols(z)]
        h_s[...] += nt(p, wi_s[:, cols(z)])
        ga_s[...] += nt(g_s[:, cols(z)], wo_s[:, cols(z)])
        pf = p.astype(jnp.float32)
        sq_s[...] += jnp.sum(pf * pf, axis=1, keepdims=True)
        return carry

    lax.fori_loop(0, chunks, first, 0)
    inv = lax.rsqrt(sq_s[...] * (1.0 / feats) + 1e-05)
    v = h_s[...] * inv
    v2 = v * v
    t = jnp.tanh(0.7978845608 * v * (1.0 + 0.044715 * v2))
    up = 0.5 * (1.0 + t)
    a = (v * up).astype(jnp.bfloat16)
    slope = up + 0.5 * v * (1.0 - t * t) * (0.7978845608 * (1.0 + 0.134145 * v2))
    b = (ga_s[...] * slope * inv).astype(jnp.bfloat16)
    act[...] = a
    gp[...] = b
    act_t[...] = a.T
    gp_t[...] = b.T

    def second(z, carry):
        wi = wi_s[:, cols(z)]
        d_s[:, cols(z)] = nn(act[...], wo_s[:, cols(z)]).astype(jnp.bfloat16)
        n_s[:, cols(z)] = nn(gp[...], wi).astype(jnp.bfloat16)
        go_s[:, cols(z)] = nn(act_t[...], g_s[:, cols(z)]).astype(jnp.bfloat16)
        gi = nn(gp_t[...], p_s[:, cols(z)])
        gi_s[:, cols(z)] = gi.astype(jnp.bfloat16)
        gain[:, cols(z)] = jnp.sum(gi * wi.astype(jnp.float32), axis=0, keepdims=True)
        for i, pair in enumerate(outs):
            at = pl.ds(i * rows, rows)
            for k, (dest, buf) in enumerate(zip(pair, (d_s, n_s))):
                pltpu.make_async_copy(
                    buf.at[at, cols(z)], dest.at[:, cols(z)], out_sem.at[k, z]
                ).start()
        for dest, which in ((g_own, core), (g_oth, 1 - core)):
            pltpu.make_async_copy(
                gi_s.at[:, w_cols(z, which)], dest.at[z, pl.ds(0, hidden), :], out_sem.at[2, z]
            ).start()
            pltpu.make_async_copy(
                go_s.at[:, w_cols(z, which)], dest.at[z, pl.ds(hidden, hidden), :], out_sem.at[3, z]
            ).start()
        return carry

    lax.fori_loop(0, chunks, second, 0)

    def drain(z, carry):
        for k, buf in enumerate((d_s, n_s, gi_s, go_s)):
            view = buf.at[:, cols(z)]
            pltpu.make_async_copy(view, view, out_sem.at[k, z]).wait()
        return carry

    lax.fori_loop(0, chunks, drain, 0)


def block(acts, w_own, w_oth):
    rows, feats = acts[0].shape
    chunks, hidden2, half = w_own.shape
    hidden = hidden2 // 2
    total = 4 * rows
    bf = jnp.bfloat16
    anywhere = pl.BlockSpec(memory_space=pl.ANY)
    flops = 12 * total * feats * hidden
    return pl.pallas_call(
        functools.partial(block_kernel, chunks),
        out_shape=[jax.ShapeDtypeStruct(act.shape, bf) for act in acts]
        + [jax.ShapeDtypeStruct(w_own.shape, bf)] * 2
        + [jax.ShapeDtypeStruct((1, feats), jnp.float32)],
        in_specs=[anywhere] * 10,
        out_specs=[anywhere] * 10 + [pl.BlockSpec(memory_space=pltpu.VMEM)],
        scratch_shapes=[pltpu.VMEM((total, feats), bf)] * 2
        + [pltpu.VMEM((hidden, feats), bf)] * 2
        + [pltpu.VMEM((total, feats), bf)] * 2
        + [pltpu.VMEM((hidden, feats), bf)] * 2
        + [pltpu.VMEM((total, hidden), jnp.float32)] * 2
        + [pltpu.VMEM((total, 1), jnp.float32)]
        + [pltpu.VMEM((total, hidden), bf)] * 2
        + [pltpu.VMEM((hidden, total), bf)] * 2
        + [pltpu.SemaphoreType.DMA((4, chunks)), pltpu.SemaphoreType.DMA((4, chunks))],
        compiler_params=pltpu.CompilerParams(vmem_limit_bytes=48 * 1024 * 1024),
        cost_estimate=pl.CostEstimate(
            flops=flops, bytes_accessed=8 * (total + hidden) * feats * 2, transcendentals=0
        ),
    )(*acts, w_own, w_oth)


def add_all(parts):
    total = parts[0].astype(jnp.float32)
    for part in parts[1:]:
        total = total + part.astype(jnp.float32)
    return total


def gather_plane(acts):
    parts = [acts] + [shift(acts, first=d) for d in (1, 2, 3)]
    p0 = jnp.concatenate([part[0] for part in parts], axis=0)
    g0 = jnp.concatenate([part[1] for part in parts], axis=0)
    p0, g0 = lax.optimization_barrier((p0, g0))
    p1, g3 = shift(p0, second=1), shift(g0, second=-1)
    g1, p3 = shift(g0, second=1), shift(p0, second=-1)
    p1, g3, g1, p3 = lax.optimization_barrier((p1, g3, g1, p3))
    p2, g2 = shift(p1, second=1), shift(g3, second=-1)
    return [p0, p1, p2, p3, g0, g1, g2, g3]


def scatter_plane(outs, gain_part, weight_part):
    d0, d1, d2, d3, n0, n1, n2, n3 = outs
    bf = jnp.bfloat16
    d2, n2 = shift(d2, second=-1), shift(n2, second=1)
    n1, d3 = shift(n1, second=-1), shift(d3, second=1)
    d2, n2, weight_part = lax.optimization_barrier((d2, n2, weight_part))
    d1, n3 = add_all([d1, d2]).astype(bf), add_all([n3, n2]).astype(bf)
    gain = pair(pair(pair(gain_part, z=1), z=2), z=4)
    d1, n3, gain = lax.optimization_barrier((d1, n3, gain))
    weight_sum = lax.psum_scatter(weight_part, "z", scatter_dimension=0, tiled=False)
    d1, n3 = shift(d1, second=-1), shift(n3, second=1)
    gain = pair(pair(gain, first=1), first=2)
    d1, d3, n1, n3, gain = lax.optimization_barrier((d1, d3, n1, n3, gain))
    both = jnp.stack([add_all([d0, d1, d3]).astype(bf), add_all([n0, n1, n3]).astype(bf)])
    rows = both.shape[1] // 4
    both = [both[:, d * rows : (d + 1) * rows] for d in range(4)]
    arrived = [shift(both[d], first=-d) for d in (1, 2, 3)] + [weight_sum]
    gain = pair(pair(pair(gain, second=1), second=2), c=1)
    *arrived, weight_sum, gain = lax.optimization_barrier([*arrived, gain])
    return add_all([both[0], *arrived]), gain, weight_sum


def pair(value, z=0, first=0, second=0, c=0):
    pairs = []
    for p in places():
        y, x = (second, first) if p[3] else (first, second)
        pairs.append((linear(*p), linear(p[0] ^ z, p[1] ^ y, p[2] ^ x, p[3] ^ c)))
    return value + lax.ppermute(value, AXES, pairs)


def shards(stream, doc_start, norm_gain, weight_in, weight_out, upstream):
    tok_rows, feats = stream.shape
    groups = tok_rows // 4
    hidden = weight_out.shape[0]
    k_rows = weight_in.shape[0]
    bf = jnp.bfloat16
    seq = lax.axis_index("z") * 2 + lax.axis_index("yl")
    gain = lax.dynamic_slice(norm_gain, (seq * k_rows,), (k_rows,))

    scaled_in = (weight_in.T.astype(jnp.float32) * gain[None, :]).astype(bf)
    both = swap_low(jnp.concatenate([scaled_in, weight_out], axis=0))
    w_own = lax.all_gather(both, "z", axis=0, tiled=False)

    starts = doc_start.reshape(groups, 4).astype(jnp.float32)
    keep = jnp.cumprod(1.0 - starts, axis=1).reshape(tok_rows)
    group_of = lax.broadcasted_iota(jnp.int32, (groups, tok_rows), 1) // 4
    here = lax.broadcasted_iota(jnp.int32, (groups, tok_rows), 0)
    pool = jnp.where(group_of == here, 0.25, 0.0).astype(bf)
    pooled = nn(pool, stream).astype(bf)
    pick = jnp.where(group_of == here, keep[None, :], 0.0).astype(bf)
    group_sums = nn(pick, upstream).astype(bf)
    following = from_behind(group_sums[:1], -1)
    grad_coarse = jnp.concatenate([group_sums[1:], following], axis=0)

    acts = jnp.stack([pooled, grad_coarse], axis=0)
    blocks = gather_plane(acts)
    w_own = lax.optimization_barrier((w_own, blocks[1], blocks[3]))[0]
    w_oth = other_core(w_own)
    results = block(blocks, w_own, w_oth)
    outs, (g_own, g_oth, gain_part) = results[:8], results[8:]

    mine = (g_own.astype(jnp.float32) + other_core(g_oth).astype(jnp.float32)).astype(bf)
    (down_sum, scaled), grad_gain, grads = scatter_plane(outs, gain_part[0] / norm_gain, mine)
    grads = swap_low(grads)
    grad_weight_in = (grads[:hidden].astype(jnp.float32) * gain[None, :]).T
    grad_weight_out = grads[hidden:].astype(jnp.float32)
    pooled_f = pooled.astype(jnp.float32)
    inv_sq = 1.0 / (jnp.mean(pooled_f * pooled_f, axis=1, keepdims=True) + 1e-05)
    coarse = (pooled_f + down_sum).astype(bf)
    carried = from_behind(coarse[groups - 1 :], 1)
    earlier = jnp.concatenate([carried, coarse[:-1]], axis=0)
    mixed_stream = (stream.astype(jnp.float32) + nn(pick.T, earlier)).astype(bf)
    grad_pooled = grad_coarse.astype(jnp.float32) + (
        scaled - pooled_f * inv_sq * jnp.mean(scaled * pooled_f, axis=1, keepdims=True)
    )
    grad_stream = (upstream.astype(jnp.float32) + nn(pool.T, grad_pooled.astype(bf))).astype(bf)
    return (mixed_stream, grad_stream, grad_gain, grad_weight_in, grad_weight_out)


def solution(mesh):
    fine = Mesh(mesh.devices.reshape(NZ, 2, NX, 2, 2), AXES)
    rows = P(AXES, None)
    seq, mp = ("z", "yl"), ("x", "yh", "c")
    in_specs = (rows, P(AXES), P(), P(seq, mp), P(mp, seq), rows)
    out_specs = (rows, rows, P(), P(seq, mp), P(mp, seq))
    return jax.shard_map(shards, mesh=fine, in_specs=in_specs, out_specs=out_specs, check_vma=False)
```
